512 devices in a mesh: dp: 64 (over y, z), expert: 8 (over x, core).
Axes of the slice: x: 4, y: 4, z: 16, core: 2. Of those that a mesh axis runs over, the one named last changes fastest.
Arguments:
- grads: bfloat16 [256, 768, 1024], P('expert', 'dp'), may hold values from -200 to 200
- momentum: float32 [256, 768, 1024], P('expert', 'dp'), may hold values from -6 to 6
Outputs:
- update: bfloat16 [256, 768, 1024], P('expert', 'dp')
- new_momentum: float32 [256, 768, 1024], P('expert', 'dp')
The draws below stay inside these ranges and needn't reach their ends.
All inputs are finite; a program needn't handle non-finite values.
Results may differ from the reference program's by a relative error of at most 0.017.
Values may be sent and summed in bfloat16 or wider, within the bound.
A program may use at most 64 MiB of HBM per device.

```python
import math
import jax
import jax.numpy as jnp
from jax import lax

H = 768
D = 1024
ITERS = 2
MATS = 32
MATS_ALL = 256
N_EXPERT = 8


def draw_grads(key, part):
    key = jax.random.fold_in(key, 5)
    first, second, third = jax.random.split(key, 3)
    shape = (MATS * N_EXPERT, H, D)
    base = jnp.clip(jax.random.normal(first, shape, jnp.float32), -6.0, 6.0)
    row_scale = jnp.exp(jax.random.uniform(second, (MATS * N_EXPERT, H, 1), jnp.float32, 0.0, math.log(10.0)))
    col_scale = jnp.exp(jax.random.uniform(third, (MATS * N_EXPERT, 1, D), jnp.float32, 0.0, math.log(10.0)))
    rise = 1.0 + 2.0 * jnp.arange(H, dtype=jnp.float32) / (H - 1)
    values = base * row_scale * col_scale * rise[None, :, None] * 0.1
    return values.astype(jnp.bfloat16)


def level_of(stream_key, shape, shards, smallest, largest):
    def one(dim, blocks):
        steps = jax.random.uniform(jax.random.fold_in(jax.random.fold_in(stream_key, 6), dim), (blocks,), jnp.float32, smallest / len(shards), largest / len(shards))
        return jnp.repeat(jnp.exp(steps), shape[dim] // blocks).reshape((-1,) + (1,) * (len(shape) - dim - 1))

    factor_of = one(*shards[0])
    for cut in shards[1:]:
        factor_of = factor_of * one(*cut)
    return factor_of


def scatter_about(own_key, dims, spread, bound, cuts=(), held_as=jnp.bfloat16):
    drawn = jax.random.normal(own_key, dims, jnp.float32) * spread
    if len(cuts) > 0:
        drawn = level_of(own_key, dims, cuts, -0.22, 0.18) * drawn
    return jnp.clip(drawn, min=-bound, max=bound).astype(held_as)


def setup_inputs(seed: int = 0) -> dict:
    seeds = jax.random.split(jax.random.key(seed), 3)
    grads = draw_grads(jax.random.fold_in(seeds[2], 71), 0)
    momentum = scatter_about(seeds[1], (MATS_ALL, H, D), 1.0, 6.0, ((0, 8), (1, 64)), jnp.float32)
    return dict(grads=grads, momentum=momentum)


A_COEF = 3.4445
B_COEF = -4.775
C_COEF = 2.0315
MOMENT = 0.95
EPS = 1e-07

def orthogonalize(sent):
    values = sent.astype(jnp.float32)
    norm = jnp.sqrt(jnp.sum(values * values))
    state = (values / (norm + EPS)).astype(jnp.bfloat16)
    for step in range(ITERS):
        gram = jnp.dot(state, state.T, preferred_element_type=jnp.float32).astype(jnp.bfloat16)
        square = jnp.dot(gram, gram, preferred_element_type=jnp.float32)
        mixer = (B_COEF * gram.astype(jnp.float32) + C_COEF * square).astype(jnp.bfloat16)
        moved = jnp.dot(mixer, state, preferred_element_type=jnp.float32)
        state = (A_COEF * state.astype(jnp.float32) + moved).astype(jnp.bfloat16)
    return state

def reference(grads, momentum):
    gradient = grads.astype(jnp.float32)
    new_momentum = MOMENT * momentum + gradient
    nesterov = (gradient + MOMENT * new_momentum).astype(jnp.bfloat16)
    ortho = lax.map(orthogonalize, nesterov)
    scale = 0.2 * math.sqrt(max(H, D))
    update = (scale * ortho.astype(jnp.float32)).astype(jnp.bfloat16)
    return (update, new_momentum)
```

```python
from functools import partial
import math

import jax
import jax.numpy as jnp
from jax import lax
from jax.experimental import pallas as pl
from jax.experimental.pallas import tpu as pltpu
from jax.sharding import PartitionSpec as P

H = 768
D = 1024
ITERS = 2

A_COEF = 3.4445
B_COEF = -4.775
C_COEF = 2.0315
MOMENT = 0.95
EPS = 1e-07

ROWS = 12
TALL = 16
MAIN = D * ROWS // TALL
EXTRA = D - MAIN
REST = TALL - ROWS
SPLITS = ROWS // REST
SIDES_Y = 4
MESH_ID = pl.DeviceIdType.MESH


def pack_rows(rows):
    tail = rows[:, MAIN:]
    below = jnp.concatenate([tail[REST * j : REST * (j + 1)] for j in range(SPLITS)], axis=1)
    return jnp.concatenate([rows[:, :MAIN], below], axis=0)


def unpack_rows(block):
    below = block[ROWS:]
    tail = jnp.concatenate(
        [below[:, EXTRA * j : EXTRA * (j + 1)] for j in range(SPLITS)], axis=0
    )
    return jnp.concatenate([block[:ROWS], tail], axis=1)


def middle_out(i, count):
    sign = 1 - 2 * (i % 2)
    return (count // 2 + sign * ((i + 1) // 2) + count) % count


def selector(plain_dim, packed_dim, shape, part):
    plain = lax.broadcasted_iota(jnp.int32, shape, plain_dim)
    packed = lax.broadcasted_iota(jnp.int32, shape, packed_dim)
    slot = (plain * 43691) >> 19
    row = plain - ROWS * slot
    if part is None:
        hit = packed == TALL * slot + row
    else:
        within = row - REST * part
        hit = (packed == TALL * slot + ROWS + within) & (within >= 0) & (within < REST)
    return jnp.where(hit, 1.0, 0.0).astype(jnp.bfloat16)


def dot(a, b):
    return jnp.dot(a, b, preferred_element_type=jnp.float32)


def dot_t(a, b):
    return lax.dot_general(a, b, (((1,), (1,)), ((), ())), preferred_element_type=jnp.float32)


def kernel(
    n_dp,
    grads_ref,
    mom_ref,
    out_ref,
    sent,
    landed,
    x0,
    x1,
    gram,
    mixer,
    away,
    home,
    sel,
    sel_t,
    sent_sem,
    landed_sem,
    away_sem,
    home_sem,
):
    n_z = n_dp // SIDES_Y
    mats = n_dp // 2
    height = ROWS * n_dp
    group = min(16, n_dp)
    plain_rows, packed_rows = ROWS * group, TALL * group
    block_rows = min(256, height)

    dp = lax.axis_index("dp")
    expert = lax.axis_index("expert")
    core = expert % 2
    y, z = dp // n_z, dp % n_z
    owns = y % 2 == core
    mine = (y // 2) * n_z + z

    def owner_of(matrix):
        return (core + 2 * (matrix // n_z)) * n_z + matrix % n_z

    barrier = pltpu.get_barrier_semaphore()

    def greet_owner(i, c):
        other = owner_of(i)

        @pl.when(other != dp)
        def _():
            pl.semaphore_signal(barrier, inc=1, device_id=(other, expert), device_id_type=MESH_ID)

        return c

    lax.fori_loop(0, mats, greet_owner, 0)

    @pl.when(owns)
    def _():
        def greet_rest(i, c):
            other = (1 - core + 2 * (i // n_z)) * n_z + i % n_z
            pl.semaphore_signal(barrier, inc=1, device_id=(other, expert), device_id_type=MESH_ID)
            return c

        lax.fori_loop(0, mats, greet_rest, 0)

    def pack_one(m, c):
        gradient = grads_ref[m].astype(jnp.float32)
        momentum = MOMENT * mom_ref[m] + gradient
        sent[m] = pack_rows(gradient + MOMENT * momentum).astype(jnp.bfloat16)
        return c

    lax.fori_loop(0, mats, pack_one, 0)

    @pl.when(owns)
    def _():
        pl.semaphore_wait(barrier, n_dp - 1)

    @pl.when(jnp.logical_not(owns))
    def _():
        pl.semaphore_wait(barrier, mats)

    def matrix_at(i):
        turn = i % (mats // 2)
        half_z = n_z // 2
        target_z = (z - z % 2 + i // (mats // 2) + 2 * middle_out(turn // 2, half_z)) % n_z
        return (turn % 2) * n_z + target_z

    def send_one(i, c):
        m = matrix_at(i)
        owner = owner_of(m)
        slot = (dp - owner + n_dp) % n_dp

        @pl.when(owner != dp)
        def _():
            pltpu.make_async_remote_copy(
                src_ref=sent.at[m],
                dst_ref=landed.at[slot],
                send_sem=sent_sem.at[m],
                recv_sem=landed_sem.at[slot],
                device_id=(owner, expert),
                device_id_type=MESH_ID,
            ).start()

        @pl.when(owner == dp)
        def _():
            pltpu.make_async_copy(sent.at[m], landed.at[0], landed_sem.at[0]).start()

        return c

    lax.fori_loop(0, mats, send_one, 0)

    @pl.when(owns)
    def _():
        for part in range(SPLITS + 1):
            which = None if part == 0 else part - 1
            sel[part] = selector(0, 1, (plain_rows, packed_rows), which)
            sel_t[part] = selector(1, 0, (packed_rows, plain_rows), which)

        def squares(slot, total):
            pltpu.make_async_copy(landed.at[slot], landed.at[slot], landed_sem.at[slot]).wait()
            values = landed[slot].astype(jnp.float32)
            return total + values * values

        total = lax.fori_loop(0, n_dp, squares, jnp.zeros((TALL, MAIN), jnp.float32))
        norm = jnp.sqrt(jnp.sum(total, axis=(0, 1), keepdims=True)) + EPS

        def unpack_group(g, c):
            block = landed[pl.ds(pl.multiple_of(g * group, group), group)]
            block = block.reshape(packed_rows, MAIN).astype(jnp.float32)
            start = (block / norm).astype(jnp.bfloat16)
            rows = pl.ds(pl.multiple_of(g * plain_rows, 16), plain_rows)
            x0[rows, :MAIN] = dot(sel[0], start).astype(jnp.bfloat16)
            tail = dot(sel[1], start[:, :EXTRA])
            for part in range(1, SPLITS):
                tail = tail + dot(sel[part + 1], start[:, EXTRA * part : EXTRA * (part + 1)])
            x0[rows, MAIN:] = tail.astype(jnp.bfloat16)
            return c

        lax.fori_loop(0, n_dp // group, unpack_group, 0)

        state = x0
        for step in range(ITERS):

            def gram_rows(r, c, state=state):
                rows = pl.ds(pl.multiple_of(r * block_rows, 16), block_rows)
                gram[rows] = dot_t(state[rows], state[...]).astype(jnp.bfloat16)
                return c

            def mixer_rows(r, c):
                rows = pl.ds(pl.multiple_of(r * block_rows, 16), block_rows)
                some = gram[rows]
                square = dot(some, gram[...])
                mixed = B_COEF * some.astype(jnp.float32) + C_COEF * square
                mixer[rows] = mixed.astype(jnp.bfloat16)
                return c

            lax.fori_loop(0, height // block_rows, gram_rows, 0)
            lax.fori_loop(0, height // block_rows, mixer_rows, 0)

            if step < ITERS - 1:

                def next_rows(r, c, state=state):
                    rows = pl.ds(pl.multiple_of(r * block_rows, 16), block_rows)
                    moved = dot(mixer[rows], state[...])
                    x1[rows] = (A_COEF * state[rows].astype(jnp.float32) + moved).astype(
                        jnp.bfloat16
                    )
                    return c

                lax.fori_loop(0, height // block_rows, next_rows, 0)
                state = x1

        scale = 0.2 * math.sqrt(max(H, D))

        def finish_group(g, c):
            rows = pl.ds(pl.multiple_of(g * plain_rows, 16), plain_rows)
            moved = dot(mixer[rows], state[...])
            ortho = (A_COEF * state[rows].astype(jnp.float32) + moved).astype(jnp.bfloat16)
            update = (scale * ortho.astype(jnp.float32)).astype(jnp.bfloat16)
            slots = pl.ds(pl.multiple_of(g * group, group), group)
            for part in range(SPLITS):
                columns = slice(EXTRA * part, EXTRA * (part + 1))
                block = dot(sel_t[0], update[:, columns]) + dot(sel_t[part + 1], update[:, MAIN:])
                away[slots, :, columns] = block.astype(jnp.bfloat16).reshape(group, TALL, EXTRA)

            def return_one(t, c):
                slot = g * group + middle_out(t, group)
                target = (dp + slot) % n_dp

                @pl.when(slot != 0)
                def _():
                    pltpu.make_async_remote_copy(
                        src_ref=away.at[slot],
                        dst_ref=home.at[mine],
                        send_sem=away_sem.at[slot],
                        recv_sem=home_sem.at[mine],
                        device_id=(target, expert),
                        device_id_type=MESH_ID,
                    ).start()

                @pl.when(slot == 0)
                def _():
                    pltpu.make_async_copy(away.at[0], home.at[mine], home_sem.at[mine]).start()

                return c

            lax.fori_loop(0, group, return_one, 0)
            return c

        lax.fori_loop(0, n_dp // group, finish_group, 0)

    def take_home(i, c):
        m = matrix_at(i)
        pltpu.make_async_copy(home.at[m], home.at[m], home_sem.at[m]).wait()
        out_ref[m] = unpack_rows(home[m].astype(jnp.float32)).astype(jnp.bfloat16)
        return c

    lax.fori_loop(0, mats, take_home, 0)

    def sent_done(m, c):
        @pl.when(owner_of(m) != dp)
        def _():
            pltpu.make_async_copy(sent.at[m], sent.at[m], sent_sem.at[m]).wait()

        return c

    lax.fori_loop(0, mats, sent_done, 0)

    @pl.when(owns)
    def _():
        def away_done(slot, c):
            pltpu.make_async_copy(away.at[slot], away.at[slot], away_sem.at[slot]).wait()
            return c

        lax.fori_loop(1, n_dp, away_done, 0)


def orthogonalized(grads, momentum, n_dp):
    mats, height = n_dp // 2, ROWS * n_dp
    group = min(16, n_dp)
    packed = lambda count: pltpu.VMEM((count, TALL, MAIN), jnp.bfloat16)
    flat = lambda *shape: pltpu.VMEM(shape, jnp.bfloat16)
    return pl.pallas_call(
        partial(kernel, n_dp),
        out_shape=jax.ShapeDtypeStruct(grads.shape, jnp.bfloat16),
        in_specs=[pl.BlockSpec(memory_space=pltpu.VMEM)] * 2,
        out_specs=pl.BlockSpec(memory_space=pltpu.VMEM),
        scratch_shapes=[
            packed(mats),
            packed(n_dp),
            flat(height, D),
            flat(height, D),
            flat(height, height),
            flat(height, height),
            packed(n_dp),
            packed(mats),
            flat(SPLITS + 1, ROWS * group, TALL * group),
            flat(SPLITS + 1, TALL * group, ROWS * group),
            pltpu.SemaphoreType.DMA((mats,)),
            pltpu.SemaphoreType.DMA((n_dp,)),
            pltpu.SemaphoreType.DMA((n_dp,)),
            pltpu.SemaphoreType.DMA((mats,)),
        ],
        compiler_params=pltpu.CompilerParams(
            collective_id=0, has_side_effects=True, vmem_limit_bytes=40 * 1024 * 1024
        ),
        cost_estimate=pl.CostEstimate(
            flops=8 * height * height * D, bytes_accessed=8 * grads.size, transcendentals=0
        ),
    )(grads, momentum)


def local(grads, momentum):
    n_dp = lax.axis_size("dp")
    update = orthogonalized(grads, momentum, n_dp)
    new_momentum = MOMENT * momentum + grads.astype(jnp.float32)
    return (update, new_momentum)


def solution(mesh):
    in_specs = (P("expert", "dp", None), P("expert", "dp", None))
    out_specs = (P("expert", "dp", None), P("expert", "dp", None))
    return jax.shard_map(local, mesh=mesh, in_specs=in_specs, out_specs=out_specs, check_vma=False)
```

```python
from functools import partial
import math

import jax
import jax.numpy as jnp
from jax import lax
from jax.experimental import pallas as pl
from jax.experimental.pallas import tpu as pltpu
from jax.sharding import PartitionSpec as P

H = 768
D = 1024
ITERS = 2

A_COEF = 3.4445
B_COEF = -4.775
C_COEF = 2.0315
MOMENT = 0.95
EPS = 1e-07

ROWS = 12
TALL = 16
MAIN = D * ROWS // TALL
EXTRA = D - MAIN
REST = TALL - ROWS
SPLITS = ROWS // REST
SIDES_Y = 4
MESH_ID = pl.DeviceIdType.MESH


def pack_rows(rows):
    tail = rows[:, MAIN:]
    below = jnp.concatenate([tail[REST * j : REST * (j + 1)] for j in range(SPLITS)], axis=1)
    return jnp.concatenate([rows[:, :MAIN], below], axis=0)


def unpack_rows(block):
    below = block[ROWS:]
    tail = jnp.concatenate(
        [below[:, EXTRA * j : EXTRA * (j + 1)] for j in range(SPLITS)], axis=0
    )
    return jnp.concatenate([block[:ROWS], tail], axis=1)


def middle_out(i, count):
    sign = 1 - 2 * (i % 2)
    return (count // 2 + sign * ((i + 1) // 2) + count) % count


def selector(plain_dim, packed_dim, shape, part):
    plain = lax.broadcasted_iota(jnp.int32, shape, plain_dim)
    packed = lax.broadcasted_iota(jnp.int32, shape, packed_dim)
    slot = (plain * 43691) >> 19
    row = plain - ROWS * slot
    if part is None:
        hit = packed == TALL * slot + row
    else:
        within = row - REST * part
        hit = (packed == TALL * slot + ROWS + within) & (within >= 0) & (within < REST)
    return jnp.where(hit, 1.0, 0.0).astype(jnp.bfloat16)


def dot(a, b):
    return jnp.dot(a, b, preferred_element_type=jnp.float32)


def dot_t(a, b):
    return lax.dot_general(a, b, (((1,), (1,)), ((), ())), preferred_element_type=jnp.float32)


def kernel(
    n_dp,
    grads_ref,
    mom_ref,
    out_ref,
    sent,
    landed,
    x0,
    x1,
    gram,
    mixer,
    away,
    home,
    sel,
    sel_t,
    sent_sem,
    landed_sem,
    away_sem,
    home_sem,
):
    n_z = n_dp // SIDES_Y
    mats = n_dp // 2
    height = ROWS * n_dp
    group = min(16, n_dp)
    plain_rows, packed_rows = ROWS * group, TALL * group
    block_rows = min(256, height)

    dp = lax.axis_index("dp")
    expert = lax.axis_index("expert")
    core = expert % 2
    y, z = dp // n_z, dp % n_z
    owns = y % 2 == core
    mine = (y // 2) * n_z + z

    def owner_of(matrix):
        return (core + 2 * (matrix // n_z)) * n_z + matrix % n_z

    barrier = pltpu.get_barrier_semaphore()

    def greet_owner(i, c):
        other = owner_of(i)

        @pl.when(other != dp)
        def _():
            pl.semaphore_signal(barrier, inc=1, device_id=(other, expert), device_id_type=MESH_ID)

        return c

    lax.fori_loop(0, mats, greet_owner, 0)

    @pl.when(owns)
    def _():
        def greet_rest(i, c):
            other = (1 - core + 2 * (i // n_z)) * n_z + i % n_z
            pl.semaphore_signal(barrier, inc=1, device_id=(other, expert), device_id_type=MESH_ID)
            return c

        lax.fori_loop(0, mats, greet_rest, 0)

    def pack_one(m, c):
        gradient = grads_ref[m].astype(jnp.float32)
        momentum = MOMENT * mom_ref[m] + gradient
        sent[m] = pack_rows(gradient + MOMENT * momentum).astype(jnp.bfloat16)
        return c

    lax.fori_loop(0, mats, pack_one, 0)

    @pl.when(owns)
    def _():
        pl.semaphore_wait(barrier, n_dp - 1)

    @pl.when(jnp.logical_not(owns))
    def _():
        pl.semaphore_wait(barrier, mats)

    def matrix_at(i):
        turn = i % (mats // 2)
        half_z = n_z // 2
        target_z = (z - z % 2 + i // (mats // 2) + 2 * middle_out(turn // 2, half_z)) % n_z
        return (turn % 2) * n_z + target_z

    def send_one(i, c):
        m = matrix_at(i)
        owner = owner_of(m)
        slot = (dp - owner + n_dp) % n_dp

        @pl.when(owner != dp)
        def _():
            pltpu.make_async_remote_copy(
                src_ref=sent.at[m],
                dst_ref=landed.at[slot],
                send_sem=sent_sem.at[m],
                recv_sem=landed_sem.at[slot],
                device_id=(owner, expert),
                device_id_type=MESH_ID,
            ).start()

        @pl.when(owner == dp)
        def _():
            pltpu.make_async_copy(sent.at[m], landed.at[0], landed_sem.at[0]).start()

        return c

    def send_done(i, c):
        m = matrix_at(i)

        @pl.when(owner_of(m) != dp)
        def _():
            pltpu.make_async_copy(sent.at[m], sent.at[m], sent_sem.at[m]).wait()

        return c

    half = mats // 2
    lax.fori_loop(0, half, send_one, 0)
    lax.fori_loop(0, half - half // 4, send_done, 0)
    lax.fori_loop(half, mats, send_one, 0)

    @pl.when(owns)
    def _():
        for part in range(SPLITS + 1):
            which = None if part == 0 else part - 1
            sel[part] = selector(0, 1, (plain_rows, packed_rows), which)
            sel_t[part] = selector(1, 0, (packed_rows, plain_rows), which)

        def squares(slot, total):
            pltpu.make_async_copy(landed.at[slot], landed.at[slot], landed_sem.at[slot]).wait()
            values = landed[slot].astype(jnp.float32)
            return total + values * values

        total = lax.fori_loop(0, n_dp, squares, jnp.zeros((TALL, MAIN), jnp.float32))
        norm = jnp.sqrt(jnp.sum(total, axis=(0, 1), keepdims=True)) + EPS

        def unpack_group(g, c):
            block = landed[pl.ds(pl.multiple_of(g * group, group), group)]
            block = block.reshape(packed_rows, MAIN).astype(jnp.float32)
            start = (block / norm).astype(jnp.bfloat16)
            rows = pl.ds(pl.multiple_of(g * plain_rows, 16), plain_rows)
            x0[rows, :MAIN] = dot(sel[0], start).astype(jnp.bfloat16)
            tail = dot(sel[1], start[:, :EXTRA])
            for part in range(1, SPLITS):
                tail = tail + dot(sel[part + 1], start[:, EXTRA * part : EXTRA * (part + 1)])
            x0[rows, MAIN:] = tail.astype(jnp.bfloat16)
            return c

        lax.fori_loop(0, n_dp // group, unpack_group, 0)

        state = x0
        for step in range(ITERS):

            def gram_rows(r, c, state=state):
                rows = pl.ds(pl.multiple_of(r * block_rows, 16), block_rows)
                gram[rows] = dot_t(state[rows], state[...]).astype(jnp.bfloat16)
                return c

            def mixer_rows(r, c):
                rows = pl.ds(pl.multiple_of(r * block_rows, 16), block_rows)
                some = gram[rows]
                square = dot(some, gram[...])
                mixed = B_COEF * some.astype(jnp.float32) + C_COEF * square
                mixer[rows] = mixed.astype(jnp.bfloat16)
                return c

            lax.fori_loop(0, height // block_rows, gram_rows, 0)
            lax.fori_loop(0, height // block_rows, mixer_rows, 0)

            if step < ITERS - 1:

                def next_rows(r, c, state=state):
                    rows = pl.ds(pl.multiple_of(r * block_rows, 16), block_rows)
                    moved = dot(mixer[rows], state[...])
                    x1[rows] = (A_COEF * state[rows].astype(jnp.float32) + moved).astype(
                        jnp.bfloat16
                    )
                    return c

                lax.fori_loop(0, height // block_rows, next_rows, 0)
                state = x1

        scale = 0.2 * math.sqrt(max(H, D))

        def finish_group(g, c):
            rows = pl.ds(pl.multiple_of(g * plain_rows, 16), plain_rows)
            moved = dot(mixer[rows], state[...])
            ortho = (A_COEF * state[rows].astype(jnp.float32) + moved).astype(jnp.bfloat16)
            update = (scale * ortho.astype(jnp.float32)).astype(jnp.bfloat16)
            slots = pl.ds(pl.multiple_of(g * group, group), group)
            for part in range(SPLITS):
                columns = slice(EXTRA * part, EXTRA * (part + 1))
                block = dot(sel_t[0], update[:, columns]) + dot(sel_t[part + 1], update[:, MAIN:])
                away[slots, :, columns] = block.astype(jnp.bfloat16).reshape(group, TALL, EXTRA)

            def return_one(t, c):
                slot = g * group + middle_out(t, group)
                target = (dp + slot) % n_dp

                @pl.when(slot != 0)
                def _():
                    pltpu.make_async_remote_copy(
                        src_ref=away.at[slot],
                        dst_ref=home.at[mine],
                        send_sem=away_sem.at[slot],
                        recv_sem=home_sem.at[mine],
                        device_id=(target, expert),
                        device_id_type=MESH_ID,
                    ).start()

                @pl.when(slot == 0)
                def _():
                    pltpu.make_async_copy(away.at[0], home.at[mine], home_sem.at[mine]).start()

                return c

            lax.fori_loop(0, group, return_one, 0)
            return c

        lax.fori_loop(0, n_dp // group, finish_group, 0)

    def take_home(i, c):
        m = matrix_at(i)
        pltpu.make_async_copy(home.at[m], home.at[m], home_sem.at[m]).wait()
        out_ref[m] = unpack_rows(home[m].astype(jnp.float32)).astype(jnp.bfloat16)
        return c

    lax.fori_loop(0, mats, take_home, 0)

    lax.fori_loop(half - half // 4, mats, send_done, 0)

    @pl.when(owns)
    def _():
        def away_done(slot, c):
            pltpu.make_async_copy(away.at[slot], away.at[slot], away_sem.at[slot]).wait()
            return c

        lax.fori_loop(1, n_dp, away_done, 0)


def orthogonalized(grads, momentum, n_dp):
    mats, height = n_dp // 2, ROWS * n_dp
    group = min(16, n_dp)
    packed = lambda count: pltpu.VMEM((count, TALL, MAIN), jnp.bfloat16)
    flat = lambda *shape: pltpu.VMEM(shape, jnp.bfloat16)
    return pl.pallas_call(
        partial(kernel, n_dp),
        out_shape=jax.ShapeDtypeStruct(grads.shape, jnp.bfloat16),
        in_specs=[pl.BlockSpec(memory_space=pltpu.VMEM)] * 2,
        out_specs=pl.BlockSpec(memory_space=pltpu.VMEM),
        scratch_shapes=[
            packed(mats),
            packed(n_dp),
            flat(height, D),
            flat(height, D),
            flat(height, height),
            flat(height, height),
            packed(n_dp),
            packed(mats),
            flat(SPLITS + 1, ROWS * group, TALL * group),
            flat(SPLITS + 1, TALL * group, ROWS * group),
            pltpu.SemaphoreType.DMA((mats,)),
            pltpu.SemaphoreType.DMA((n_dp,)),
            pltpu.SemaphoreType.DMA((n_dp,)),
            pltpu.SemaphoreType.DMA((mats,)),
        ],
        compiler_params=pltpu.CompilerParams(
            collective_id=0, has_side_effects=True, vmem_limit_bytes=40 * 1024 * 1024
        ),
        cost_estimate=pl.CostEstimate(
            flops=8 * height * height * D, bytes_accessed=8 * grads.size, transcendentals=0
        ),
    )(grads, momentum)


def local(grads, momentum):
    n_dp = lax.axis_size("dp")
    update = orthogonalized(grads, momentum, n_dp)
    new_momentum = MOMENT * momentum + grads.astype(jnp.float32)
    return (update, new_momentum)


def solution(mesh):
    in_specs = (P("expert", "dp", None), P("expert", "dp", None))
    out_specs = (P("expert", "dp", None), P("expert", "dp", None))
    return jax.shard_map(local, mesh=mesh, in_specs=in_specs, out_specs=out_specs, check_vma=False)
```

```python
from functools import partial
import math

import jax
import jax.numpy as jnp
from jax import lax
from jax.experimental import pallas as pl
from jax.experimental.pallas import tpu as pltpu
from jax.sharding import PartitionSpec as P

H = 768
D = 1024
ITERS = 2

A_COEF = 3.4445
B_COEF = -4.775
C_COEF = 2.0315
MOMENT = 0.95
EPS = 1e-07

ROWS = 12
TALL = 16
MAIN = D * ROWS // TALL
EXTRA = D - MAIN
REST = TALL - ROWS
SPLITS = ROWS // REST
SIDES_Y = 4
MESH_ID = pl.DeviceIdType.MESH


def pack_rows(rows):
    tail = rows[:, MAIN:]
    below = jnp.concatenate([tail[REST * j : REST * (j + 1)] for j in range(SPLITS)], axis=1)
    return jnp.concatenate([rows[:, :MAIN], below], axis=0)


def unpack_rows(block):
    below = block[ROWS:]
    tail = jnp.concatenate(
        [below[:, EXTRA * j : EXTRA * (j + 1)] for j in range(SPLITS)], axis=0
    )
    return jnp.concatenate([block[:ROWS], tail], axis=1)


def middle_out(i, count):
    sign = 1 - 2 * (i % 2)
    return (count // 2 + sign * ((i + 1) // 2) + count) % count


def selector(plain_dim, packed_dim, shape, part):
    plain = lax.broadcasted_iota(jnp.int32, shape, plain_dim)
    packed = lax.broadcasted_iota(jnp.int32, shape, packed_dim)
    slot = (plain * 43691) >> 19
    row = plain - ROWS * slot
    if part is None:
        hit = packed == TALL * slot + row
    else:
        within = row - REST * part
        hit = (packed == TALL * slot + ROWS + within) & (within >= 0) & (within < REST)
    return jnp.where(hit, 1.0, 0.0).astype(jnp.bfloat16)


def dot(a, b):
    return jnp.dot(a, b, preferred_element_type=jnp.float32)


def dot_t(a, b):
    return lax.dot_general(a, b, (((1,), (1,)), ((), ())), preferred_element_type=jnp.float32)


def kernel(
    n_dp,
    grads_ref,
    mom_ref,
    out_ref,
    sent,
    landed,
    x0,
    x1,
    gram,
    mixer,
    away,
    home,
    sel,
    sel_t,
    via,
    back,
    sent_sem,
    landed_sem,
    away_sem,
    home_sem,
    via_sem,
    via_sent_sem,
    back_sem,
    back_sent_sem,
):
    n_z = n_dp // SIDES_Y
    mats = n_dp // 2
    height = ROWS * n_dp
    group = min(16, n_dp)
    plain_rows, packed_rows = ROWS * group, TALL * group
    block_rows = 256 if height % 256 == 0 else plain_rows

    dp = lax.axis_index("dp")
    expert = lax.axis_index("expert")
    core = expert % 2
    y, z = dp // n_z, dp % n_z
    owns = y % 2 == core
    mine = (y // 2) * n_z + z

    def owner_of(matrix):
        return (core + 2 * (matrix // n_z)) * n_z + matrix % n_z

    barrier = pltpu.get_barrier_semaphore()

    def greet_owner(i, c):
        other = owner_of(i)

        @pl.when(other != dp)
        def _():
            pl.semaphore_signal(barrier, inc=1, device_id=(other, expert), device_id_type=MESH_ID)

        return c

    lax.fori_loop(0, mats, greet_owner, 0)

    @pl.when(owns)
    def _():
        def greet_rest(i, c):
            other = (1 - core + 2 * (i // n_z)) * n_z + i % n_z
            pl.semaphore_signal(barrier, inc=1, device_id=(other, expert), device_id_type=MESH_ID)
            return c

        lax.fori_loop(0, mats, greet_rest, 0)

    def pack_one(m, c):
        gradient = grads_ref[m].astype(jnp.float32)
        momentum = MOMENT * mom_ref[m] + gradient
        sent[m] = pack_rows(gradient + MOMENT * momentum).astype(jnp.bfloat16)
        return c

    lax.fori_loop(0, mats, pack_one, 0)

    @pl.when(owns)
    def _():
        pl.semaphore_wait(barrier, n_dp - 1)

    @pl.when(jnp.logical_not(owns))
    def _():
        pl.semaphore_wait(barrier, mats)

    def matrix_at(i):
        turn = i % (mats // 2)
        half_z = n_z // 2
        target_z = (z - z % 2 + i // (mats // 2) + 2 * middle_out(turn // 2, half_z)) % n_z
        return (turn % 2) * n_z + target_z

    quarter = n_z // 4

    def copy_to(target, src, dst, send_sem, recv_sem):
        return pltpu.make_async_remote_copy(
            src_ref=src,
            dst_ref=dst,
            send_sem=send_sem,
            recv_sem=recv_sem,
            device_id=(target, expert),
            device_id_type=MESH_ID,
        )

    def relay_z(rises):
        return (z + jnp.where(rises, quarter, n_z - quarter)) % n_z

    def send_far(turn, c):
        m = turn * n_z + (z + n_z // 2) % n_z
        relay = (core + 2 * turn) * n_z + relay_z((z // 2 + turn) % 2 == 0)
        copy_to(relay, sent.at[m], via.at[y], sent_sem.at[m], via_sem.at[y]).start()
        return c

    lax.fori_loop(0, 2, send_far, 0)

    def send_one(i, c):
        m = matrix_at(i)
        owner = owner_of(m)
        slot = (dp - owner + n_dp) % n_dp
        far = (owner - dp + n_dp) % n_z == n_z // 2

        @pl.when((owner != dp) & jnp.logical_not(far))
        def _():
            copy_to(
                owner, sent.at[m], landed.at[slot], sent_sem.at[m], landed_sem.at[slot]
            ).start()

        @pl.when(owner == dp)
        def _():
            pltpu.make_async_copy(sent.at[m], landed.at[0], landed_sem.at[0]).start()

        return c

    lax.fori_loop(0, mats // 4, send_one, 0)

    @pl.when(owns)
    def _():
        rises = ((z + n_z - quarter) // 2 + y // 2) % 2 == 0
        source_z = (z + jnp.where(rises, n_z - quarter, quarter)) % n_z
        owner = y * n_z + relay_z(rises)

        def pass_on(source_y, c):
            slot = (source_y * n_z + source_z - owner + n_dp) % n_dp
            block = via.at[source_y]
            pltpu.make_async_copy(block, block, via_sem.at[source_y]).wait()
            copy_to(
                owner, block, landed.at[slot], via_sent_sem.at[source_y], landed_sem.at[slot]
            ).start()
            return c

        lax.fori_loop(0, SIDES_Y, pass_on, 0)

    lax.fori_loop(mats // 4, mats, send_one, 0)

    @pl.when(owns)
    def _():
        for part in range(SPLITS + 1):
            which = None if part == 0 else part - 1
            sel[part] = selector(0, 1, (plain_rows, packed_rows), which)
            sel_t[part] = selector(1, 0, (packed_rows, plain_rows), which)

        def squares(slot, total):
            pltpu.make_async_copy(landed.at[slot], landed.at[slot], landed_sem.at[slot]).wait()
            values = landed[slot].astype(jnp.float32)
            return total + values * values

        total = lax.fori_loop(0, n_dp, squares, jnp.zeros((TALL, MAIN), jnp.float32))
        norm = jnp.sqrt(jnp.sum(total, axis=(0, 1), keepdims=True)) + EPS

        def unpack_group(g, c):
            block = landed[pl.ds(pl.multiple_of(g * group, group), group)]
            block = block.reshape(packed_rows, MAIN).astype(jnp.float32)
            start = (block / norm).astype(jnp.bfloat16)
            rows = pl.ds(pl.multiple_of(g * plain_rows, 16), plain_rows)
            x0[rows, :MAIN] = dot(sel[0], start).astype(jnp.bfloat16)
            tail = dot(sel[1], start[:, :EXTRA])
            for part in range(1, SPLITS):
                tail = tail + dot(sel[part + 1], start[:, EXTRA * part : EXTRA * (part + 1)])
            x0[rows, MAIN:] = tail.astype(jnp.bfloat16)
            return c

        lax.fori_loop(0, n_dp // group, unpack_group, 0)

        state = x0
        for step in range(ITERS):

            def gram_rows(r, c, state=state):
                rows = pl.ds(pl.multiple_of(r * block_rows, 16), block_rows)
                gram[rows] = dot_t(state[rows], state[...]).astype(jnp.bfloat16)
                return c

            def mixer_rows(r, c):
                rows = pl.ds(pl.multiple_of(r * block_rows, 16), block_rows)
                some = gram[rows]
                square = dot(some, gram[...])
                mixed = B_COEF * some.astype(jnp.float32) + C_COEF * square
                mixer[rows] = mixed.astype(jnp.bfloat16)
                return c

            lax.fori_loop(0, height // block_rows, gram_rows, 0)
            lax.fori_loop(0, height // block_rows, mixer_rows, 0)

            if step < ITERS - 1:

                def next_rows(r, c, state=state):
                    rows = pl.ds(pl.multiple_of(r * block_rows, 16), block_rows)
                    moved = dot(mixer[rows], state[...])
                    x1[rows] = (A_COEF * state[rows].astype(jnp.float32) + moved).astype(
                        jnp.bfloat16
                    )
                    return c

                lax.fori_loop(0, height // block_rows, next_rows, 0)
                state = x1

        scale = 0.2 * math.sqrt(max(H, D))

        def finish_group(g, c):
            rows = pl.ds(pl.multiple_of(g * plain_rows, 16), plain_rows)
            moved = dot(mixer[rows], state[...])
            ortho = (A_COEF * state[rows].astype(jnp.float32) + moved).astype(jnp.bfloat16)
            update = (scale * ortho.astype(jnp.float32)).astype(jnp.bfloat16)
            slots = pl.ds(pl.multiple_of(g * group, group), group)
            for part in range(SPLITS):
                columns = slice(EXTRA * part, EXTRA * (part + 1))
                block = dot(sel_t[0], update[:, columns]) + dot(sel_t[part + 1], update[:, MAIN:])
                away[slots, :, columns] = block.astype(jnp.bfloat16).reshape(group, TALL, EXTRA)

            def return_one(t, c):
                slot = g * group + middle_out(t, group)
                target = (dp + slot) % n_dp
                target_y = target // n_z
                far = slot % n_z == n_z // 2

                @pl.when((slot != 0) & jnp.logical_not(far))
                def _():
                    copy_to(
                        target, away.at[slot], home.at[mine], away_sem.at[slot], home_sem.at[mine]
                    ).start()

                @pl.when(far)
                def _():
                    relay = y * n_z + relay_z((z // 2 + target_y) % 2 == 0)
                    copy_to(
                        relay,
                        away.at[slot],
                        back.at[target_y],
                        away_sem.at[slot],
                        back_sem.at[target_y],
                    ).start()

                @pl.when(slot == 0)
                def _():
                    pltpu.make_async_copy(away.at[0], home.at[mine], home_sem.at[mine]).start()

                return c

            lax.fori_loop(0, group, return_one, 0)
            return c

        lax.fori_loop(0, n_dp // group, finish_group, 0)

        def pass_back(target_y, c):
            rises = ((z + n_z - quarter) // 2 + target_y) % 2 == 0
            owner_z = (z + jnp.where(rises, n_z - quarter, quarter)) % n_z
            m = (y // 2) * n_z + owner_z
            target = target_y * n_z + relay_z(rises)
            block = back.at[target_y]
            pltpu.make_async_copy(block, block, back_sem.at[target_y]).wait()
            copy_to(
                target, block, home.at[m], back_sent_sem.at[target_y], home_sem.at[m]
            ).start()
            return c

        lax.fori_loop(0, SIDES_Y, pass_back, 0)

    def take_home(i, c):
        m = matrix_at(i)
        pltpu.make_async_copy(home.at[m], home.at[m], home_sem.at[m]).wait()
        out_ref[m] = unpack_rows(home[m].astype(jnp.float32)).astype(jnp.bfloat16)
        return c

    lax.fori_loop(0, mats, take_home, 0)

    def sent_done(m, c):
        @pl.when(owner_of(m) != dp)
        def _():
            pltpu.make_async_copy(sent.at[m], sent.at[m], sent_sem.at[m]).wait()

        return c

    lax.fori_loop(0, mats, sent_done, 0)

    @pl.when(owns)
    def _():
        def away_done(slot, c):
            pltpu.make_async_copy(away.at[slot], away.at[slot], away_sem.at[slot]).wait()
            return c

        lax.fori_loop(1, n_dp, away_done, 0)

        def passed(side, c):
            pltpu.make_async_copy(via.at[side], via.at[side], via_sent_sem.at[side]).wait()
            pltpu.make_async_copy(back.at[side], back.at[side], back_sent_sem.at[side]).wait()
            return c

        lax.fori_loop(0, SIDES_Y, passed, 0)


def orthogonalized(grads, momentum, n_dp):
    mats, height = n_dp // 2, ROWS * n_dp
    group = min(16, n_dp)
    packed = lambda count: pltpu.VMEM((count, TALL, MAIN), jnp.bfloat16)
    flat = lambda *shape: pltpu.VMEM(shape, jnp.bfloat16)
    return pl.pallas_call(
        partial(kernel, n_dp),
        out_shape=jax.ShapeDtypeStruct(grads.shape, jnp.bfloat16),
        in_specs=[pl.BlockSpec(memory_space=pltpu.VMEM)] * 2,
        out_specs=pl.BlockSpec(memory_space=pltpu.VMEM),
        scratch_shapes=[
            packed(mats),
            packed(n_dp),
            flat(height, D),
            flat(height, D),
            flat(height, height),
            flat(height, height),
            packed(n_dp),
            packed(mats),
            flat(SPLITS + 1, ROWS * group, TALL * group),
            flat(SPLITS + 1, TALL * group, ROWS * group),
            packed(SIDES_Y),
            packed(SIDES_Y),
            pltpu.SemaphoreType.DMA((mats,)),
            pltpu.SemaphoreType.DMA((n_dp,)),
            pltpu.SemaphoreType.DMA((n_dp,)),
            pltpu.SemaphoreType.DMA((mats,)),
            *[pltpu.SemaphoreType.DMA((SIDES_Y,))] * 4,
        ],
        compiler_params=pltpu.CompilerParams(
            collective_id=0, has_side_effects=True, vmem_limit_bytes=40 * 1024 * 1024
        ),
        cost_estimate=pl.CostEstimate(
            flops=8 * height * height * D, bytes_accessed=8 * grads.size, transcendentals=0
        ),
    )(grads, momentum)


def local(grads, momentum):
    n_dp = lax.axis_size("dp")
    update = orthogonalized(grads, momentum, n_dp)
    new_momentum = MOMENT * momentum + grads.astype(jnp.float32)
    return (update, new_momentum)


def solution(mesh):
    in_specs = (P("expert", "dp", None), P("expert", "dp", None))
    out_specs = (P("expert", "dp", None), P("expert", "dp", None))
    return jax.shard_map(local, mesh=mesh, in_specs=in_specs, out_specs=out_specs, check_vma=False)
```

```python
from functools import partial
import math

import jax
import jax.numpy as jnp
from jax import lax
from jax.experimental import pallas as pl
from jax.experimental.pallas import tpu as pltpu
from jax.sharding import PartitionSpec as P

H = 768
D = 1024
ITERS = 2

A_COEF = 3.4445
B_COEF = -4.775
C_COEF = 2.0315
MOMENT = 0.95
EPS = 1e-07

ROWS = 12
TALL = 16
MAIN = D * ROWS // TALL
EXTRA = D - MAIN
REST = TALL - ROWS
SPLITS = ROWS // REST
SIDES_Y = 4
BATCHES = 4
MESH_ID = pl.DeviceIdType.MESH


def pack_rows(rows):
    tail = rows[:, MAIN:]
    below = jnp.concatenate([tail[REST * j : REST * (j + 1)] for j in range(SPLITS)], axis=1)
    return jnp.concatenate([rows[:, :MAIN], below], axis=0)


def unpack_rows(block):
    below = block[ROWS:]
    tail = jnp.concatenate(
        [below[:, EXTRA * j : EXTRA * (j + 1)] for j in range(SPLITS)], axis=0
    )
    return jnp.concatenate([block[:ROWS], tail], axis=1)


def middle_out(i, count):
    sign = 1 - 2 * (i % 2)
    return (count // 2 + sign * ((i + 1) // 2) + count) % count


def selector(plain_dim, packed_dim, shape, part):
    plain = lax.broadcasted_iota(jnp.int32, shape, plain_dim)
    packed = lax.broadcasted_iota(jnp.int32, shape, packed_dim)
    slot = (plain * 43691) >> 19
    row = plain - ROWS * slot
    if part is None:
        hit = packed == TALL * slot + row
    else:
        within = row - REST * part
        hit = (packed == TALL * slot + ROWS + within) & (within >= 0) & (within < REST)
    return jnp.where(hit, 1.0, 0.0).astype(jnp.bfloat16)


def dot(a, b):
    return jnp.dot(a, b, preferred_element_type=jnp.float32)


def dot_t(a, b):
    return lax.dot_general(a, b, (((1,), (1,)), ((), ())), preferred_element_type=jnp.float32)


def kernel(
    n_dp,
    grads_ref,
    mom_ref,
    out_ref,
    sent,
    landed,
    x0,
    x1,
    gram,
    mixer,
    away,
    home,
    sel,
    sel_t,
    sent_sem,
    landed_sem,
    away_sem,
    home_sem,
):
    n_z = n_dp // SIDES_Y
    mats = n_dp // 2
    height = ROWS * n_dp
    group = min(16, n_dp)
    plain_rows, packed_rows = ROWS * group, TALL * group
    block_rows = 256 if height % 256 == 0 else plain_rows

    dp = lax.axis_index("dp")
    expert = lax.axis_index("expert")
    core = expert % 2
    y, z = dp // n_z, dp % n_z
    owns = y % 2 == core
    mine = (y // 2) * n_z + z

    def owner_of(matrix):
        return (core + 2 * (matrix // n_z)) * n_z + matrix % n_z

    barrier = pltpu.get_barrier_semaphore()

    def greet_owner(i, c):
        other = owner_of(i)

        @pl.when(other != dp)
        def _():
            pl.semaphore_signal(barrier, inc=1, device_id=(other, expert), device_id_type=MESH_ID)

        return c

    lax.fori_loop(0, mats, greet_owner, 0)

    @pl.when(owns)
    def _():
        def greet_rest(i, c):
            other = (1 - core + 2 * (i // n_z)) * n_z + i % n_z
            pl.semaphore_signal(barrier, inc=1, device_id=(other, expert), device_id_type=MESH_ID)
            return c

        lax.fori_loop(0, mats, greet_rest, 0)

    def pack_one(m, c):
        gradient = grads_ref[m].astype(jnp.float32)
        momentum = MOMENT * mom_ref[m] + gradient
        sent[m] = pack_rows(gradient + MOMENT * momentum).astype(jnp.bfloat16)
        return c

    lax.fori_loop(0, mats, pack_one, 0)

    @pl.when(owns)
    def _():
        pl.semaphore_wait(barrier, n_dp - 1)

    @pl.when(jnp.logical_not(owns))
    def _():
        pl.semaphore_wait(barrier, mats)

    def matrix_at(i):
        batch, turn = i // (mats // BATCHES), i % (mats // BATCHES)
        side = turn % 2
        first_z = z - z % BATCHES + (batch + core + 2 * side) % BATCHES
        return side * n_z + (first_z + BATCHES * middle_out(turn // 2, n_z // BATCHES)) % n_z

    def send_one(i, c):
        m = matrix_at(i)
        owner = owner_of(m)
        slot = (dp - owner + n_dp) % n_dp

        @pl.when(owner != dp)
        def _():
            pltpu.make_async_remote_copy(
                src_ref=sent.at[m],
                dst_ref=landed.at[slot],
                send_sem=sent_sem.at[m],
                recv_sem=landed_sem.at[slot],
                device_id=(owner, expert),
                device_id_type=MESH_ID,
            ).start()

        @pl.when(owner == dp)
        def _():
            pltpu.make_async_copy(sent.at[m], landed.at[0], landed_sem.at[0]).start()

        return c

    lax.fori_loop(0, mats, send_one, 0)

    @pl.when(owns)
    def _():
        for part in range(SPLITS + 1):
            which = None if part == 0 else part - 1
            sel[part] = selector(0, 1, (plain_rows, packed_rows), which)
            sel_t[part] = selector(1, 0, (packed_rows, plain_rows), which)

        def squares(slot, total):
            pltpu.make_async_copy(landed.at[slot], landed.at[slot], landed_sem.at[slot]).wait()
            values = landed[slot].astype(jnp.float32)
            return total + values * values

        total = lax.fori_loop(0, n_dp, squares, jnp.zeros((TALL, MAIN), jnp.float32))
        norm = jnp.sqrt(jnp.sum(total, axis=(0, 1), keepdims=True)) + EPS

        def unpack_group(g, c):
            block = landed[pl.ds(pl.multiple_of(g * group, group), group)]
            block = block.reshape(packed_rows, MAIN).astype(jnp.float32)
            start = (block / norm).astype(jnp.bfloat16)
            rows = pl.ds(pl.multiple_of(g * plain_rows, 16), plain_rows)
            x0[rows, :MAIN] = dot(sel[0], start).astype(jnp.bfloat16)
            tail = dot(sel[1], start[:, :EXTRA])
            for part in range(1, SPLITS):
                tail = tail + dot(sel[part + 1], start[:, EXTRA * part : EXTRA * (part + 1)])
            x0[rows, MAIN:] = tail.astype(jnp.bfloat16)
            return c

        lax.fori_loop(0, n_dp // group, unpack_group, 0)

        state = x0
        for step in range(ITERS):

            def gram_rows(r, c, state=state):
                rows = pl.ds(pl.multiple_of(r * block_rows, 16), block_rows)
                gram[rows] = dot_t(state[rows], state[...]).astype(jnp.bfloat16)
                return c

            def mixer_rows(r, c):
                rows = pl.ds(pl.multiple_of(r * block_rows, 16), block_rows)
                some = gram[rows]
                square = dot(some, gram[...])
                mixed = B_COEF * some.astype(jnp.float32) + C_COEF * square
                mixer[rows] = mixed.astype(jnp.bfloat16)
                return c

            lax.fori_loop(0, height // block_rows, gram_rows, 0)
            lax.fori_loop(0, height // block_rows, mixer_rows, 0)

            if step < ITERS - 1:

                def next_rows(r, c, state=state):
                    rows = pl.ds(pl.multiple_of(r * block_rows, 16), block_rows)
                    moved = dot(mixer[rows], state[...])
                    x1[rows] = (A_COEF * state[rows].astype(jnp.float32) + moved).astype(
                        jnp.bfloat16
                    )
                    return c

                lax.fori_loop(0, height // block_rows, next_rows, 0)
                state = x1

        scale = 0.2 * math.sqrt(max(H, D))

        def finish_group(g, c):
            rows = pl.ds(pl.multiple_of(g * plain_rows, 16), plain_rows)
            moved = dot(mixer[rows], state[...])
            ortho = (A_COEF * state[rows].astype(jnp.float32) + moved).astype(jnp.bfloat16)
            update = (scale * ortho.astype(jnp.float32)).astype(jnp.bfloat16)
            slots = pl.ds(pl.multiple_of(g * group, group), group)
            for part in range(SPLITS):
                columns = slice(EXTRA * part, EXTRA * (part + 1))
                block = dot(sel_t[0], update[:, columns]) + dot(sel_t[part + 1], update[:, MAIN:])
                away[slots, :, columns] = block.astype(jnp.bfloat16).reshape(group, TALL, EXTRA)

            def return_one(t, c):
                slot = g * group + middle_out(t, group)
                target = (dp + slot) % n_dp

                @pl.when(slot != 0)
                def _():
                    pltpu.make_async_remote_copy(
                        src_ref=away.at[slot],
                        dst_ref=home.at[mine],
                        send_sem=away_sem.at[slot],
                        recv_sem=home_sem.at[mine],
                        device_id=(target, expert),
                        device_id_type=MESH_ID,
                    ).start()

                @pl.when(slot == 0)
                def _():
                    pltpu.make_async_copy(away.at[0], home.at[mine], home_sem.at[mine]).start()

                return c

            lax.fori_loop(0, group, return_one, 0)
            return c

        lax.fori_loop(0, n_dp // group, finish_group, 0)

    def take_home(i, c):
        m = matrix_at(i)
        pltpu.make_async_copy(home.at[m], home.at[m], home_sem.at[m]).wait()
        out_ref[m] = unpack_rows(home[m].astype(jnp.float32)).astype(jnp.bfloat16)
        return c

    lax.fori_loop(0, mats, take_home, 0)

    def sent_done(m, c):
        @pl.when(owner_of(m) != dp)
        def _():
            pltpu.make_async_copy(sent.at[m], sent.at[m], sent_sem.at[m]).wait()

        return c

    lax.fori_loop(0, mats, sent_done, 0)

    @pl.when(owns)
    def _():
        def away_done(slot, c):
            pltpu.make_async_copy(away.at[slot], away.at[slot], away_sem.at[slot]).wait()
            return c

        lax.fori_loop(1, n_dp, away_done, 0)


def orthogonalized(grads, momentum, n_dp):
    mats, height = n_dp // 2, ROWS * n_dp
    group = min(16, n_dp)
    packed = lambda count: pltpu.VMEM((count, TALL, MAIN), jnp.bfloat16)
    flat = lambda *shape: pltpu.VMEM(shape, jnp.bfloat16)
    return pl.pallas_call(
        partial(kernel, n_dp),
        out_shape=jax.ShapeDtypeStruct(grads.shape, jnp.bfloat16),
        in_specs=[pl.BlockSpec(memory_space=pltpu.VMEM)] * 2,
        out_specs=pl.BlockSpec(memory_space=pltpu.VMEM),
        scratch_shapes=[
            packed(mats),
            packed(n_dp),
            flat(height, D),
            flat(height, D),
            flat(height, height),
            flat(height, height),
            packed(n_dp),
            packed(mats),
            flat(SPLITS + 1, ROWS * group, TALL * group),
            flat(SPLITS + 1, TALL * group, ROWS * group),
            pltpu.SemaphoreType.DMA((mats,)),
            pltpu.SemaphoreType.DMA((n_dp,)),
            pltpu.SemaphoreType.DMA((n_dp,)),
            pltpu.SemaphoreType.DMA((mats,)),
        ],
        compiler_params=pltpu.CompilerParams(
            collective_id=0, has_side_effects=True, vmem_limit_bytes=40 * 1024 * 1024
        ),
        cost_estimate=pl.CostEstimate(
            flops=8 * height * height * D, bytes_accessed=8 * grads.size, transcendentals=0
        ),
    )(grads, momentum)


def local(grads, momentum):
    n_dp = lax.axis_size("dp")
    update = orthogonalized(grads, momentum, n_dp)
    new_momentum = MOMENT * momentum + grads.astype(jnp.float32)
    return (update, new_momentum)


def solution(mesh):
    in_specs = (P("expert", "dp", None), P("expert", "dp", None))
    out_specs = (P("expert", "dp", None), P("expert", "dp", None))
    return jax.shard_map(local, mesh=mesh, in_specs=in_specs, out_specs=out_specs, check_vma=False)
```

```python
from functools import partial
import math

import jax
import jax.numpy as jnp
from jax import lax
from jax.experimental import pallas as pl
from jax.experimental.pallas import tpu as pltpu
from jax.sharding import PartitionSpec as P

H = 768
D = 1024
ITERS = 2

A_COEF = 3.4445
B_COEF = -4.775
C_COEF = 2.0315
MOMENT = 0.95
EPS = 1e-07

ROWS = 12
TALL = 16
MAIN = D * ROWS // TALL
EXTRA = D - MAIN
LANES = 128
REST = TALL - ROWS
SPLITS = ROWS // REST
SIDES_Y = 4
BATCHES = 4
MESH_ID = pl.DeviceIdType.MESH


def rows_of(ref, tile, matrix, mats):
    return ref.at[tile, pl.ds(matrix, ROWS, stride=mats), :]


def pack_rows(tiles):
    for tile in range(MAIN // LANES):
        part, side = tile // 2, tile % 2
        below = tiles[MAIN // LANES + side][REST * part : REST * (part + 1)]
        yield jnp.concatenate([tiles[tile], below], axis=0)


def unpack_rows(tiles):
    for tile in range(MAIN // LANES):
        yield tiles[tile][:ROWS]
    for side in range(EXTRA // LANES):
        yield jnp.concatenate([tiles[2 * part + side][ROWS:] for part in range(SPLITS)], axis=0)


def middle_out(i, count):
    sign = 1 - 2 * (i % 2)
    return (count // 2 + sign * ((i + 1) // 2) + count) % count


def selector(plain_dim, packed_dim, shape, part):
    plain = lax.broadcasted_iota(jnp.int32, shape, plain_dim)
    packed = lax.broadcasted_iota(jnp.int32, shape, packed_dim)
    slot = (plain * 43691) >> 19
    row = plain - ROWS * slot
    if part is None:
        hit = packed == TALL * slot + row
    else:
        within = row - REST * part
        hit = (packed == TALL * slot + ROWS + within) & (within >= 0) & (within < REST)
    return jnp.where(hit, 1.0, 0.0).astype(jnp.bfloat16)


def dot(a, b):
    return jnp.dot(a, b, preferred_element_type=jnp.float32)


def dot_t(a, b):
    return lax.dot_general(a, b, (((1,), (1,)), ((), ())), preferred_element_type=jnp.float32)


def kernel(
    n_dp,
    grads_ref,
    mom_ref,
    out_ref,
    new_mom_ref,
    rows32,
    sent,
    landed,
    x0,
    x1,
    gram,
    mixer,
    away,
    home,
    sel,
    sel_t,
    sent_sem,
    landed_sem,
    away_sem,
    home_sem,
):
    n_z = n_dp // SIDES_Y
    mats = n_dp // 2
    height = ROWS * n_dp
    group = min(16, n_dp)
    plain_rows, packed_rows = ROWS * group, TALL * group
    block_rows = 256 if height % 256 == 0 else plain_rows

    dp = lax.axis_index("dp")
    expert = lax.axis_index("expert")
    core = expert % 2
    y, z = dp // n_z, dp % n_z
    owns = y % 2 == core
    mine = (y // 2) * n_z + z

    def owner_of(matrix):
        return (core + 2 * (matrix // n_z)) * n_z + matrix % n_z

    barrier = pltpu.get_barrier_semaphore()

    def greet_owner(i, c):
        other = owner_of(i)

        @pl.when(other != dp)
        def _():
            pl.semaphore_signal(barrier, inc=1, device_id=(other, expert), device_id_type=MESH_ID)

        return c

    lax.fori_loop(0, mats, greet_owner, 0)

    @pl.when(owns)
    def _():
        def greet_rest(i, c):
            other = (1 - core + 2 * (i // n_z)) * n_z + i % n_z
            pl.semaphore_signal(barrier, inc=1, device_id=(other, expert), device_id_type=MESH_ID)
            return c

        lax.fori_loop(0, mats, greet_rest, 0)

    def momentum_row(i, c):
        gradient = grads_ref[i].astype(jnp.float32)
        momentum = MOMENT * mom_ref[i] + gradient
        new_mom_ref[i] = momentum
        nesterov = gradient + MOMENT * momentum
        here = pl.ds(pl.multiple_of(i * mats, 8), mats)
        for tile in range(D // LANES):
            rows32[tile, here, :] = nesterov[:, LANES * tile : LANES * (tile + 1)]
        return c

    lax.fori_loop(0, ROWS, momentum_row, 0)

    @pl.when(owns)
    def _():
        pl.semaphore_wait(barrier, n_dp - 1)

    @pl.when(jnp.logical_not(owns))
    def _():
        pl.semaphore_wait(barrier, mats)

    def matrix_at(i):
        batch, turn = i // (mats // BATCHES), i % (mats // BATCHES)
        side = turn % 2
        first_z = z - z % BATCHES + (batch + core + 2 * side) % BATCHES
        return side * n_z + (first_z + BATCHES * middle_out(turn // 2, n_z // BATCHES)) % n_z

    def send_one(i, c):
        m = matrix_at(i)
        owner = owner_of(m)
        slot = (dp - owner + n_dp) % n_dp
        tiles = [rows_of(rows32, tile, m, mats)[...] for tile in range(D // LANES)]
        for tile, block in enumerate(pack_rows(tiles)):
            sent[m, :, LANES * tile : LANES * (tile + 1)] = block.astype(jnp.bfloat16)

        @pl.when(owner != dp)
        def _():
            pltpu.make_async_remote_copy(
                src_ref=sent.at[m],
                dst_ref=landed.at[slot],
                send_sem=sent_sem.at[m],
                recv_sem=landed_sem.at[slot],
                device_id=(owner, expert),
                device_id_type=MESH_ID,
            ).start()

        @pl.when(owner == dp)
        def _():
            pltpu.make_async_copy(sent.at[m], landed.at[0], landed_sem.at[0]).start()

        return c

    lax.fori_loop(0, mats, send_one, 0)

    @pl.when(owns)
    def _():
        for part in range(SPLITS + 1):
            which = None if part == 0 else part - 1
            sel[part] = selector(0, 1, (plain_rows, packed_rows), which)
            sel_t[part] = selector(1, 0, (packed_rows, plain_rows), which)

        def squares(slot, total):
            pltpu.make_async_copy(landed.at[slot], landed.at[slot], landed_sem.at[slot]).wait()
            values = landed[slot].astype(jnp.float32)
            return total + values * values

        total = lax.fori_loop(0, n_dp, squares, jnp.zeros((TALL, MAIN), jnp.float32))
        norm = jnp.sqrt(jnp.sum(total, axis=(0, 1), keepdims=True)) + EPS

        def unpack_group(g, c):
            block = landed[pl.ds(pl.multiple_of(g * group, group), group)]
            block = block.reshape(packed_rows, MAIN).astype(jnp.float32)
            start = (block / norm).astype(jnp.bfloat16)
            rows = pl.ds(pl.multiple_of(g * plain_rows, 16), plain_rows)
            x0[rows, :MAIN] = dot(sel[0], start).astype(jnp.bfloat16)
            tail = dot(sel[1], start[:, :EXTRA])
            for part in range(1, SPLITS):
                tail = tail + dot(sel[part + 1], start[:, EXTRA * part : EXTRA * (part + 1)])
            x0[rows, MAIN:] = tail.astype(jnp.bfloat16)
            return c

        lax.fori_loop(0, n_dp // group, unpack_group, 0)

        state = x0
        for step in range(ITERS):

            def gram_rows(r, c, state=state):
                rows = pl.ds(pl.multiple_of(r * block_rows, 16), block_rows)
                gram[rows] = dot_t(state[rows], state[...]).astype(jnp.bfloat16)
                return c

            def mixer_rows(r, c):
                rows = pl.ds(pl.multiple_of(r * block_rows, 16), block_rows)
                some = gram[rows]
                square = dot(some, gram[...])
                mixed = B_COEF * some.astype(jnp.float32) + C_COEF * square
                mixer[rows] = mixed.astype(jnp.bfloat16)
                return c

            lax.fori_loop(0, height // block_rows, gram_rows, 0)
            lax.fori_loop(0, height // block_rows, mixer_rows, 0)

            if step < ITERS - 1:

                def next_rows(r, c, state=state):
                    rows = pl.ds(pl.multiple_of(r * block_rows, 16), block_rows)
                    moved = dot(mixer[rows], state[...])
                    x1[rows] = (A_COEF * state[rows].astype(jnp.float32) + moved).astype(
                        jnp.bfloat16
                    )
                    return c

                lax.fori_loop(0, height // block_rows, next_rows, 0)
                state = x1

        scale = 0.2 * math.sqrt(max(H, D))

        def finish_group(g, c):
            rows = pl.ds(pl.multiple_of(g * plain_rows, 16), plain_rows)
            moved = dot(mixer[rows], state[...])
            ortho = (A_COEF * state[rows].astype(jnp.float32) + moved).astype(jnp.bfloat16)
            update = (scale * ortho.astype(jnp.float32)).astype(jnp.bfloat16)
            slots = pl.ds(pl.multiple_of(g * group, group), group)
            for part in range(SPLITS):
                columns = slice(EXTRA * part, EXTRA * (part + 1))
                block = dot(sel_t[0], update[:, columns]) + dot(sel_t[part + 1], update[:, MAIN:])
                away[slots, :, columns] = block.astype(jnp.bfloat16).reshape(group, TALL, EXTRA)

            def return_one(t, c):
                slot = g * group + middle_out(t, group)
                target = (dp + slot) % n_dp

                @pl.when(slot != 0)
                def _():
                    pltpu.make_async_remote_copy(
                        src_ref=away.at[slot],
                        dst_ref=home.at[mine],
                        send_sem=away_sem.at[slot],
                        recv_sem=home_sem.at[mine],
                        device_id=(target, expert),
                        device_id_type=MESH_ID,
                    ).start()

                @pl.when(slot == 0)
                def _():
                    pltpu.make_async_copy(away.at[0], home.at[mine], home_sem.at[mine]).start()

                return c

            lax.fori_loop(0, group, return_one, 0)
            return c

        lax.fori_loop(0, n_dp // group, finish_group, 0)

    def take_home(i, c):
        m = matrix_at(i)
        pltpu.make_async_copy(home.at[m], home.at[m], home_sem.at[m]).wait()
        block = home[m].astype(jnp.float32)
        tiles = [block[:, LANES * tile : LANES * (tile + 1)] for tile in range(MAIN // LANES)]
        for tile, rows in enumerate(unpack_rows(tiles)):
            rows_of(rows32, tile, m, mats)[...] = rows
        return c

    lax.fori_loop(0, mats, take_home, 0)

    def update_row(i, c):
        here = pl.ds(pl.multiple_of(i * mats, 8), mats)
        for tile in range(D // LANES):
            columns = slice(LANES * tile, LANES * (tile + 1))
            out_ref[i, :, columns] = rows32[tile, here, :].astype(jnp.bfloat16)
        return c

    lax.fori_loop(0, ROWS, update_row, 0)

    def sent_done(m, c):
        @pl.when(owner_of(m) != dp)
        def _():
            pltpu.make_async_copy(sent.at[m], sent.at[m], sent_sem.at[m]).wait()

        return c

    lax.fori_loop(0, mats, sent_done, 0)

    @pl.when(owns)
    def _():
        def away_done(slot, c):
            pltpu.make_async_copy(away.at[slot], away.at[slot], away_sem.at[slot]).wait()
            return c

        lax.fori_loop(1, n_dp, away_done, 0)


def orthogonalized(grads, momentum, n_dp):
    mats, height = n_dp // 2, ROWS * n_dp
    group = min(16, n_dp)
    packed = lambda count: pltpu.VMEM((count, TALL, MAIN), jnp.bfloat16)
    flat = lambda *shape: pltpu.VMEM(shape, jnp.bfloat16)
    return pl.pallas_call(
        partial(kernel, n_dp),
        out_shape=[
            jax.ShapeDtypeStruct(grads.shape, jnp.bfloat16),
            jax.ShapeDtypeStruct(grads.shape, jnp.float32),
        ],
        in_specs=[pl.BlockSpec(memory_space=pltpu.VMEM)] * 2,
        out_specs=[pl.BlockSpec(memory_space=pltpu.VMEM)] * 2,
        scratch_shapes=[
            pltpu.VMEM((D // LANES, ROWS * mats, LANES), jnp.float32),
            packed(mats),
            packed(n_dp),
            flat(height, D),
            flat(height, D),
            flat(height, height),
            flat(height, height),
            packed(n_dp),
            packed(mats),
            flat(SPLITS + 1, ROWS * group, TALL * group),
            flat(SPLITS + 1, TALL * group, ROWS * group),
            pltpu.SemaphoreType.DMA((mats,)),
            pltpu.SemaphoreType.DMA((n_dp,)),
            pltpu.SemaphoreType.DMA((n_dp,)),
            pltpu.SemaphoreType.DMA((mats,)),
        ],
        compiler_params=pltpu.CompilerParams(
            collective_id=0, has_side_effects=True, vmem_limit_bytes=40 * 1024 * 1024
        ),
        cost_estimate=pl.CostEstimate(
            flops=8 * height * height * D, bytes_accessed=8 * grads.size, transcendentals=0
        ),
    )(grads, momentum)


def local(grads, momentum):
    n_dp = lax.axis_size("dp")
    swap = lambda array: jnp.transpose(array, (1, 0, 2))
    update, new_momentum = orthogonalized(swap(grads), swap(momentum), n_dp)
    return (swap(update), swap(new_momentum))


def solution(mesh):
    in_specs = (P("expert", "dp", None), P("expert", "dp", None))
    out_specs = (P("expert", "dp", None), P("expert", "dp", None))
    return jax.shard_map(local, mesh=mesh, in_specs=in_specs, out_specs=out_specs, check_vma=False)
```

```python
from functools import partial
import math

import jax
import jax.numpy as jnp
from jax import lax
from jax.experimental import pallas as pl
from jax.experimental.pallas import tpu as pltpu
from jax.sharding import PartitionSpec as P

H = 768
D = 1024
ITERS = 2

A_COEF = 3.4445
B_COEF = -4.775
C_COEF = 2.0315
MOMENT = 0.95
EPS = 1e-07

ROWS = 12
TALL = 16
MAIN = D * ROWS // TALL
EXTRA = D - MAIN
LANES = 128
REST = TALL - ROWS
SPLITS = ROWS // REST
SIDES_Y = 4
BATCHES = 4
EARLY = 3
MESH_ID = pl.DeviceIdType.MESH


def rows_of(ref, tile, matrix, mats):
    return ref.at[tile, pl.ds(matrix, ROWS, stride=mats), :]


def pack_rows(tiles):
    for tile in range(MAIN // LANES):
        part, side = tile // 2, tile % 2
        below = tiles[MAIN // LANES + side][REST * part : REST * (part + 1)]
        yield jnp.concatenate([tiles[tile], below], axis=0)


def unpack_rows(tiles):
    for tile in range(MAIN // LANES):
        yield tiles[tile][:ROWS]
    for side in range(EXTRA // LANES):
        yield jnp.concatenate([tiles[2 * part + side][ROWS:] for part in range(SPLITS)], axis=0)


def middle_out(i, count):
    sign = 1 - 2 * (i % 2)
    return (count // 2 + sign * ((i + 1) // 2) + count) % count


def selector(plain_dim, packed_dim, shape, part):
    plain = lax.broadcasted_iota(jnp.int32, shape, plain_dim)
    packed = lax.broadcasted_iota(jnp.int32, shape, packed_dim)
    slot = (plain * 43691) >> 19
    row = plain - ROWS * slot
    if part is None:
        hit = packed == TALL * slot + row
    else:
        within = row - REST * part
        hit = (packed == TALL * slot + ROWS + within) & (within >= 0) & (within < REST)
    return jnp.where(hit, 1.0, 0.0).astype(jnp.bfloat16)


def dot(a, b):
    return jnp.dot(a, b, preferred_element_type=jnp.float32)


def dot_t(a, b):
    return lax.dot_general(a, b, (((1,), (1,)), ((), ())), preferred_element_type=jnp.float32)


def kernel(
    n_dp,
    grads_ref,
    mom_ref,
    out_ref,
    new_mom_ref,
    rows32,
    sent,
    landed,
    x0,
    x1,
    gram,
    mixer,
    away,
    home,
    sel,
    sel_t,
    via,
    back,
    sent_sem,
    landed_sem,
    away_sem,
    home_sem,
    via_sem,
    via_sent_sem,
    back_sem,
    back_sent_sem,
):
    n_z = n_dp // SIDES_Y
    mats = n_dp // 2
    height = ROWS * n_dp
    group = min(16, n_dp)
    plain_rows, packed_rows = ROWS * group, TALL * group
    block_rows = 256 if height % 256 == 0 else plain_rows

    dp = lax.axis_index("dp")
    expert = lax.axis_index("expert")
    core = expert % 2
    y, z = dp // n_z, dp % n_z
    owns = y % 2 == core
    mine = (y // 2) * n_z + z
    quarter = n_z // 4

    def along_z(rises):
        return (z + jnp.where(rises, quarter, n_z - quarter)) % n_z

    def copy_to(target, src, dst, send_sem, recv_sem):
        return pltpu.make_async_remote_copy(
            src_ref=src,
            dst_ref=dst,
            send_sem=send_sem,
            recv_sem=recv_sem,
            device_id=(target, expert),
            device_id_type=MESH_ID,
        )

    def owner_of(matrix):
        return (core + 2 * (matrix // n_z)) * n_z + matrix % n_z

    barrier = pltpu.get_barrier_semaphore()

    def greet_owner(i, c):
        other = owner_of(i)

        @pl.when(other != dp)
        def _():
            pl.semaphore_signal(barrier, inc=1, device_id=(other, expert), device_id_type=MESH_ID)

        return c

    lax.fori_loop(0, mats, greet_owner, 0)

    @pl.when(owns)
    def _():
        def greet_rest(i, c):
            other = (1 - core + 2 * (i // n_z)) * n_z + i % n_z
            pl.semaphore_signal(barrier, inc=1, device_id=(other, expert), device_id_type=MESH_ID)
            return c

        lax.fori_loop(0, mats, greet_rest, 0)

    @pl.when(jnp.logical_not(owns))
    def _():
        for rises in (True, False):
            other = y * n_z + along_z(rises)
            pl.semaphore_signal(barrier, inc=1, device_id=(other, expert), device_id_type=MESH_ID)

    def momentum_row(i, c):
        gradient = grads_ref[i].astype(jnp.float32)
        momentum = MOMENT * mom_ref[i] + gradient
        new_mom_ref[i] = momentum
        nesterov = gradient + MOMENT * momentum
        here = pl.ds(pl.multiple_of(i * mats, 8), mats)
        for tile in range(D // LANES):
            rows32[tile, here, :] = nesterov[:, LANES * tile : LANES * (tile + 1)]
        return c

    lax.fori_loop(0, ROWS, momentum_row, 0)

    @pl.when(owns)
    def _():
        pl.semaphore_wait(barrier, n_dp - 1)

    @pl.when(jnp.logical_not(owns))
    def _():
        pl.semaphore_wait(barrier, mats + 2)

    def matrix_at(i):
        batch, turn = i // (mats // BATCHES), i % (mats // BATCHES)
        side = turn % 2
        first_z = z - z % BATCHES + (batch + core + 2 * side) % BATCHES
        return side * n_z + (first_z + BATCHES * middle_out(turn // 2, n_z // BATCHES)) % n_z

    def pack_one(m):
        tiles = [rows_of(rows32, tile, m, mats)[...] for tile in range(D // LANES)]
        for tile, block in enumerate(pack_rows(tiles)):
            sent[m, :, LANES * tile : LANES * (tile + 1)] = block.astype(jnp.bfloat16)

    def send_far(turn, c):
        m = turn * n_z + (z + n_z // 2) % n_z
        relay = (core + 2 * turn) * n_z + along_z((z // 2 + turn) % 2 == 0)
        pack_one(m)
        copy_to(relay, sent.at[m], via.at[y], sent_sem.at[m], via_sem.at[y]).start()
        return c

    lax.fori_loop(0, 2, send_far, 0)

    def send_one(i, c):
        m = matrix_at(i)
        owner = owner_of(m)
        slot = (dp - owner + n_dp) % n_dp
        far = m % n_z == (z + n_z // 2) % n_z

        @pl.when((owner != dp) & jnp.logical_not(far))
        def _():
            pack_one(m)
            copy_to(
                owner, sent.at[m], landed.at[slot], sent_sem.at[m], landed_sem.at[slot]
            ).start()

        @pl.when(owner == dp)
        def _():
            pack_one(m)
            pltpu.make_async_copy(sent.at[m], landed.at[0], landed_sem.at[0]).start()

        return c

    lax.fori_loop(0, EARLY, send_one, 0)

    @pl.when(owns)
    def _():
        rises = ((z + n_z - quarter) // 2 + y // 2) % 2 == 0
        source_z = along_z(jnp.logical_not(rises))
        owner = y * n_z + along_z(rises)

        def pass_on(source_y, c):
            slot = (source_y * n_z + source_z - owner + n_dp) % n_dp
            block = via.at[source_y]
            pltpu.make_async_copy(block, block, via_sem.at[source_y]).wait()
            copy_to(
                owner, block, landed.at[slot], via_sent_sem.at[source_y], landed_sem.at[slot]
            ).start()
            return c

        lax.fori_loop(0, SIDES_Y, pass_on, 0)

    lax.fori_loop(EARLY, mats, send_one, 0)

    @pl.when(owns)
    def _():
        for part in range(SPLITS + 1):
            which = None if part == 0 else part - 1
            sel[part] = selector(0, 1, (plain_rows, packed_rows), which)
            sel_t[part] = selector(1, 0, (packed_rows, plain_rows), which)

        def squares(slot, total):
            pltpu.make_async_copy(landed.at[slot], landed.at[slot], landed_sem.at[slot]).wait()
            values = landed[slot].astype(jnp.float32)
            return total + values * values

        total = lax.fori_loop(0, n_dp, squares, jnp.zeros((TALL, MAIN), jnp.float32))
        norm = jnp.sqrt(jnp.sum(total, axis=(0, 1), keepdims=True)) + EPS

        def unpack_group(g, c):
            block = landed[pl.ds(pl.multiple_of(g * group, group), group)]
            block = block.reshape(packed_rows, MAIN).astype(jnp.float32)
            start = (block / norm).astype(jnp.bfloat16)
            rows = pl.ds(pl.multiple_of(g * plain_rows, 16), plain_rows)
            x0[rows, :MAIN] = dot(sel[0], start).astype(jnp.bfloat16)
            tail = dot(sel[1], start[:, :EXTRA])
            for part in range(1, SPLITS):
                tail = tail + dot(sel[part + 1], start[:, EXTRA * part : EXTRA * (part + 1)])
            x0[rows, MAIN:] = tail.astype(jnp.bfloat16)
            return c

        lax.fori_loop(0, n_dp // group, unpack_group, 0)

        state = x0
        for step in range(ITERS):

            def gram_rows(r, c, state=state):
                rows = pl.ds(pl.multiple_of(r * block_rows, 16), block_rows)
                gram[rows] = dot_t(state[rows], state[...]).astype(jnp.bfloat16)
                return c

            def mixer_rows(r, c):
                rows = pl.ds(pl.multiple_of(r * block_rows, 16), block_rows)
                some = gram[rows]
                square = dot(some, gram[...])
                mixed = B_COEF * some.astype(jnp.float32) + C_COEF * square
                mixer[rows] = mixed.astype(jnp.bfloat16)
                return c

            lax.fori_loop(0, height // block_rows, gram_rows, 0)
            lax.fori_loop(0, height // block_rows, mixer_rows, 0)

            if step < ITERS - 1:

                def next_rows(r, c, state=state):
                    rows = pl.ds(pl.multiple_of(r * block_rows, 16), block_rows)
                    moved = dot(mixer[rows], state[...])
                    x1[rows] = (A_COEF * state[rows].astype(jnp.float32) + moved).astype(
                        jnp.bfloat16
                    )
                    return c

                lax.fori_loop(0, height // block_rows, next_rows, 0)
                state = x1

        scale = 0.2 * math.sqrt(max(H, D))

        def finish_group(g, c):
            rows = pl.ds(pl.multiple_of(g * plain_rows, 16), plain_rows)
            moved = dot(mixer[rows], state[...])
            ortho = (A_COEF * state[rows].astype(jnp.float32) + moved).astype(jnp.bfloat16)
            update = (scale * ortho.astype(jnp.float32)).astype(jnp.bfloat16)
            slots = pl.ds(pl.multiple_of(g * group, group), group)
            for part in range(SPLITS):
                columns = slice(EXTRA * part, EXTRA * (part + 1))
                block = dot(sel_t[0], update[:, columns]) + dot(sel_t[part + 1], update[:, MAIN:])
                away[slots, :, columns] = block.astype(jnp.bfloat16).reshape(group, TALL, EXTRA)

            def return_one(t, c):
                slot = g * group + middle_out(t, group)
                target = (dp + slot) % n_dp
                target_y = target // n_z
                far = slot % n_z == n_z // 2

                @pl.when((slot != 0) & jnp.logical_not(far))
                def _():
                    copy_to(
                        target, away.at[slot], home.at[mine], away_sem.at[slot], home_sem.at[mine]
                    ).start()

                @pl.when(far)
                def _():
                    shift = (target_y + 1 + core) % 2
                    relay_y = (target_y + shift) % SIDES_Y
                    relay = relay_y * n_z + along_z((z // 2 + target_y) % 2 == 0)
                    place = 2 * (y // 2) + shift
                    copy_to(
                        relay,
                        away.at[slot],
                        back.at[place],
                        away_sem.at[slot],
                        back_sem.at[place],
                    ).start()

                @pl.when(slot == 0)
                def _():
                    pltpu.make_async_copy(away.at[0], home.at[mine], home_sem.at[mine]).start()

                return c

            lax.fori_loop(0, group, return_one, 0)
            return c

        lax.fori_loop(0, n_dp // group, finish_group, 0)

    @pl.when(jnp.logical_not(owns))
    def _():
        flip = ((z + 2 * SIDES_Y - core) % SIDES_Y) // 2

        def pass_back(i, c):
            half, shift = (i // 2 + flip) % 2, i % 2
            target_y = (y + SIDES_Y - shift) % SIDES_Y
            rises = ((z + n_z - quarter) // 2 + target_y) % 2 == 0
            m = half * n_z + along_z(jnp.logical_not(rises))
            target = target_y * n_z + along_z(rises)
            place = 2 * half + shift
            block = back.at[place]
            pltpu.make_async_copy(block, block, back_sem.at[place]).wait()
            copy_to(target, block, home.at[m], back_sent_sem.at[place], home_sem.at[m]).start()
            return c

        lax.fori_loop(0, SIDES_Y, pass_back, 0)

    def take_home(i, c):
        m = matrix_at(i)
        pltpu.make_async_copy(home.at[m], home.at[m], home_sem.at[m]).wait()
        block = home[m].astype(jnp.float32)
        tiles = [block[:, LANES * tile : LANES * (tile + 1)] for tile in range(MAIN // LANES)]
        for tile, rows in enumerate(unpack_rows(tiles)):
            rows_of(rows32, tile, m, mats)[...] = rows
        return c

    lax.fori_loop(0, mats, take_home, 0)

    def update_row(i, c):
        here = pl.ds(pl.multiple_of(i * mats, 8), mats)
        for tile in range(D // LANES):
            columns = slice(LANES * tile, LANES * (tile + 1))
            out_ref[i, :, columns] = rows32[tile, here, :].astype(jnp.bfloat16)
        return c

    lax.fori_loop(0, ROWS, update_row, 0)

    def sent_done(m, c):
        @pl.when(owner_of(m) != dp)
        def _():
            pltpu.make_async_copy(sent.at[m], sent.at[m], sent_sem.at[m]).wait()

        return c

    lax.fori_loop(0, mats, sent_done, 0)

    @pl.when(owns)
    def _():
        def away_done(slot, c):
            pltpu.make_async_copy(away.at[slot], away.at[slot], away_sem.at[slot]).wait()
            return c

        lax.fori_loop(1, n_dp, away_done, 0)

        def passed_on(side, c):
            pltpu.make_async_copy(via.at[side], via.at[side], via_sent_sem.at[side]).wait()
            return c

        lax.fori_loop(0, SIDES_Y, passed_on, 0)

    @pl.when(jnp.logical_not(owns))
    def _():
        def passed_back(side, c):
            pltpu.make_async_copy(back.at[side], back.at[side], back_sent_sem.at[side]).wait()
            return c

        lax.fori_loop(0, SIDES_Y, passed_back, 0)


def orthogonalized(grads, momentum, n_dp):
    mats, height = n_dp // 2, ROWS * n_dp
    group = min(16, n_dp)
    packed = lambda count: pltpu.VMEM((count, TALL, MAIN), jnp.bfloat16)
    flat = lambda *shape: pltpu.VMEM(shape, jnp.bfloat16)
    return pl.pallas_call(
        partial(kernel, n_dp),
        out_shape=[
            jax.ShapeDtypeStruct(grads.shape, jnp.bfloat16),
            jax.ShapeDtypeStruct(grads.shape, jnp.float32),
        ],
        in_specs=[pl.BlockSpec(memory_space=pltpu.VMEM)] * 2,
        out_specs=[pl.BlockSpec(memory_space=pltpu.VMEM)] * 2,
        scratch_shapes=[
            pltpu.VMEM((D // LANES, ROWS * mats, LANES), jnp.float32),
            packed(mats),
            packed(n_dp),
            flat(height, D),
            flat(height, D),
            flat(height, height),
            flat(height, height),
            packed(n_dp),
            packed(mats),
            flat(SPLITS + 1, ROWS * group, TALL * group),
            flat(SPLITS + 1, TALL * group, ROWS * group),
            packed(SIDES_Y),
            packed(SIDES_Y),
            pltpu.SemaphoreType.DMA((mats,)),
            pltpu.SemaphoreType.DMA((n_dp,)),
            pltpu.SemaphoreType.DMA((n_dp,)),
            pltpu.SemaphoreType.DMA((mats,)),
            *[pltpu.SemaphoreType.DMA((SIDES_Y,))] * 4,
        ],
        compiler_params=pltpu.CompilerParams(
            collective_id=0, has_side_effects=True, vmem_limit_bytes=40 * 1024 * 1024
        ),
        cost_estimate=pl.CostEstimate(
            flops=8 * height * height * D, bytes_accessed=8 * grads.size, transcendentals=0
        ),
    )(grads, momentum)


def local(grads, momentum):
    n_dp = lax.axis_size("dp")
    swap = lambda array: jnp.transpose(array, (1, 0, 2))
    update, new_momentum = orthogonalized(swap(grads), swap(momentum), n_dp)
    return (swap(update), swap(new_momentum))


def solution(mesh):
    in_specs = (P("expert", "dp", None), P("expert", "dp", None))
    out_specs = (P("expert", "dp", None), P("expert", "dp", None))
    return jax.shard_map(local, mesh=mesh, in_specs=in_specs, out_specs=out_specs, check_vma=False)
```

```python
from functools import partial
import math

import jax
import jax.numpy as jnp
from jax import lax
from jax.experimental import pallas as pl
from jax.experimental.pallas import tpu as pltpu
from jax.sharding import PartitionSpec as P

H = 768
D = 1024
ITERS = 2

A_COEF = 3.4445
B_COEF = -4.775
C_COEF = 2.0315
MOMENT = 0.95
EPS = 1e-07

ROWS = 12
TALL = 16
MAIN = D * ROWS // TALL
EXTRA = D - MAIN
LANES = 128
REST = TALL - ROWS
SPLITS = ROWS // REST
SIDES_Y = 4
BATCHES = 4
VMEM_MIB = 62
MESH_ID = pl.DeviceIdType.MESH


def rows_of(ref, tile, matrix, mats):
    return ref.at[tile, pl.ds(matrix, ROWS, stride=mats), :]


def pack_rows(tiles):
    for tile in range(MAIN // LANES):
        part, side = tile // 2, tile % 2
        below = tiles[MAIN // LANES + side][REST * part : REST * (part + 1)]
        yield jnp.concatenate([tiles[tile], below], axis=0)


def unpack_rows(tiles):
    for tile in range(MAIN // LANES):
        yield tiles[tile][:ROWS]
    for side in range(EXTRA // LANES):
        yield jnp.concatenate([tiles[2 * part + side][ROWS:] for part in range(SPLITS)], axis=0)


def middle_out(i, count):
    sign = 1 - 2 * (i % 2)
    return (count // 2 + sign * ((i + 1) // 2) + count) % count


def selector(plain_dim, packed_dim, shape, part):
    plain = lax.broadcasted_iota(jnp.int32, shape, plain_dim)
    packed = lax.broadcasted_iota(jnp.int32, shape, packed_dim)
    slot = (plain * 43691) >> 19
    row = plain - ROWS * slot
    if part is None:
        hit = packed == TALL * slot + row
    else:
        within = row - REST * part
        hit = (packed == TALL * slot + ROWS + within) & (within >= 0) & (within < REST)
    return jnp.where(hit, 1.0, 0.0).astype(jnp.bfloat16)


def dot(a, b):
    return jnp.dot(a, b, preferred_element_type=jnp.float32)


def dot_t(a, b):
    return lax.dot_general(a, b, (((1,), (1,)), ((), ())), preferred_element_type=jnp.float32)


def kernel(
    n_dp,
    grads_hbm,
    mom_hbm,
    out_ref,
    new_mom_hbm,
    grads_ref,
    mom_ref,
    rows32,
    sent,
    landed,
    x0,
    x1,
    gram,
    mixer,
    away,
    home,
    sel,
    sel_t,
    sent_sem,
    landed_sem,
    away_sem,
    home_sem,
    read_sem,
    write_sem,
):
    n_z = n_dp // SIDES_Y
    mats = n_dp // 2
    height = ROWS * n_dp
    group = min(16, n_dp)
    plain_rows, packed_rows = ROWS * group, TALL * group
    block = 256 if height % 256 == 0 else 128

    dp = lax.axis_index("dp")
    expert = lax.axis_index("expert")
    core = expert % 2
    y, z = dp // n_z, dp % n_z
    owns = y % 2 == core
    mine = (y // 2) * n_z + z

    def owner_of(matrix):
        return (core + 2 * (matrix // n_z)) * n_z + matrix % n_z

    def read(i):
        yield pltpu.make_async_copy(mom_hbm.at[i], mom_ref.at[i], read_sem.at[0, i])
        yield pltpu.make_async_copy(grads_hbm.at[i], grads_ref.at[i], read_sem.at[1, i])

    def write(i):
        return pltpu.make_async_copy(mom_ref.at[i], new_mom_hbm.at[i], write_sem.at[i])

    def start_read(i, c):
        for copy in read(i):
            copy.start()
        return c

    lax.fori_loop(0, ROWS, start_read, 0)

    barrier = pltpu.get_barrier_semaphore()

    def greet_owner(i, c):
        other = owner_of(i)

        @pl.when(other != dp)
        def _():
            pl.semaphore_signal(barrier, inc=1, device_id=(other, expert), device_id_type=MESH_ID)

        return c

    lax.fori_loop(0, mats, greet_owner, 0)

    @pl.when(owns)
    def _():
        def greet_rest(i, c):
            other = (1 - core + 2 * (i // n_z)) * n_z + i % n_z
            pl.semaphore_signal(barrier, inc=1, device_id=(other, expert), device_id_type=MESH_ID)
            return c

        lax.fori_loop(0, mats, greet_rest, 0)

    def momentum_row(i, c):
        for copy in read(i):
            copy.wait()
        gradient = grads_ref[i].astype(jnp.float32)
        momentum = MOMENT * mom_ref[i] + gradient
        mom_ref[i] = momentum
        write(i).start()
        nesterov = gradient + MOMENT * momentum
        here = pl.ds(pl.multiple_of(i * mats, 8), mats)
        for tile in range(D // LANES):
            rows32[tile, here, :] = nesterov[:, LANES * tile : LANES * (tile + 1)]
        return c

    lax.fori_loop(0, ROWS, momentum_row, 0)

    @pl.when(owns)
    def _():
        pl.semaphore_wait(barrier, n_dp - 1)

    @pl.when(jnp.logical_not(owns))
    def _():
        pl.semaphore_wait(barrier, mats)

    def matrix_at(i):
        batch, turn = i // (mats // BATCHES), i % (mats // BATCHES)
        each = n_z // BATCHES
        side = (turn // each + (y + SIDES_Y - core) % SIDES_Y // 2) % 2
        first_z = z - z % BATCHES + (batch + core + 2 * side) % BATCHES
        return side * n_z + (first_z + BATCHES * middle_out(turn % each, each)) % n_z

    def send_one(i, c):
        m = matrix_at(i)
        owner = owner_of(m)
        slot = (dp - owner + n_dp) % n_dp
        tiles = [rows_of(rows32, tile, m, mats)[...] for tile in range(D // LANES)]
        for tile, block in enumerate(pack_rows(tiles)):
            sent[m, :, LANES * tile : LANES * (tile + 1)] = block.astype(jnp.bfloat16)

        @pl.when(owner != dp)
        def _():
            pltpu.make_async_remote_copy(
                src_ref=sent.at[m],
                dst_ref=landed.at[slot],
                send_sem=sent_sem.at[m],
                recv_sem=landed_sem.at[slot],
                device_id=(owner, expert),
                device_id_type=MESH_ID,
            ).start()

        @pl.when(owner == dp)
        def _():
            pltpu.make_async_copy(sent.at[m], landed.at[0], landed_sem.at[0]).start()

        return c

    lax.fori_loop(0, mats, send_one, 0)

    @pl.when(owns)
    def _():
        for part in range(SPLITS + 1):
            which = None if part == 0 else part - 1
            sel[part] = selector(0, 1, (plain_rows, packed_rows), which)
            sel_t[part] = selector(1, 0, (packed_rows, plain_rows), which)

        def unpack_group(g, total):
            def squares(t, total):
                slot = g * group + t
                block = landed.at[slot]
                pltpu.make_async_copy(block, block, landed_sem.at[slot]).wait()
                values = block[...].astype(jnp.float32)
                return total + values * values

            total = lax.fori_loop(0, group, squares, total)
            block = landed[pl.ds(pl.multiple_of(g * group, group), group)]
            block = block.reshape(packed_rows, MAIN)
            rows = pl.ds(pl.multiple_of(g * plain_rows, 16), plain_rows)
            x0[rows, :MAIN] = dot(sel[0], block).astype(jnp.bfloat16)
            tail = dot(sel[1], block[:, :EXTRA])
            for part in range(1, SPLITS):
                tail = tail + dot(sel[part + 1], block[:, EXTRA * part : EXTRA * (part + 1)])
            x0[rows, MAIN:] = tail.astype(jnp.bfloat16)
            return total

        total = jnp.zeros((TALL, MAIN), jnp.float32)
        total = lax.fori_loop(0, n_dp // group, unpack_group, total)
        norm = jnp.sqrt(jnp.sum(total, axis=(0, 1), keepdims=True)) + EPS
        scale_in = 1.0 / norm

        def start_rows(r, c):
            rows = pl.ds(pl.multiple_of(r * plain_rows, 16), plain_rows)
            x0[rows] = (x0[rows].astype(jnp.float32) * scale_in).astype(jnp.bfloat16)
            return c

        lax.fori_loop(0, n_dp // group, start_rows, 0)

        state = x0
        for step in range(ITERS):

            def gram_columns(r, c, state=state):
                part = pl.ds(pl.multiple_of(r * block, 128), block)
                gram[:, part] = dot_t(state[...], state[part]).astype(jnp.bfloat16)
                return c

            def mixer_columns(r, c):
                part = pl.ds(pl.multiple_of(r * block, 128), block)
                some = gram[:, part]
                mixed = B_COEF * some.astype(jnp.float32) + C_COEF * dot(gram[...], some)
                mixer[:, part] = mixed.astype(jnp.bfloat16)
                return c

            lax.fori_loop(0, height // block, gram_columns, 0)
            lax.fori_loop(0, height // block, mixer_columns, 0)

            if step < ITERS - 1:

                def next_columns(r, c, state=state):
                    part = pl.ds(pl.multiple_of(r * block, 128), block)
                    some = state[:, part]
                    moved = dot(mixer[...], some)
                    x1[:, part] = (A_COEF * some.astype(jnp.float32) + moved).astype(jnp.bfloat16)
                    return c

                lax.fori_loop(0, D // block, next_columns, 0)
                state = x1

        scale = 0.2 * math.sqrt(max(H, D))

        def finish_group(g, c):
            rows = pl.ds(pl.multiple_of(g * plain_rows, 16), plain_rows)
            moved = dot(mixer[rows], state[...])
            ortho = (A_COEF * state[rows].astype(jnp.float32) + moved).astype(jnp.bfloat16)
            update = (scale * ortho.astype(jnp.float32)).astype(jnp.bfloat16)
            slots = pl.ds(pl.multiple_of(g * group, group), group)
            for part in range(SPLITS):
                columns = slice(EXTRA * part, EXTRA * (part + 1))
                block = dot(sel_t[0], update[:, columns]) + dot(sel_t[part + 1], update[:, MAIN:])
                away[slots, :, columns] = block.astype(jnp.bfloat16).reshape(group, TALL, EXTRA)

            def return_one(t, c):
                slot = g * group + middle_out(t, group)
                target = (dp + slot) % n_dp

                @pl.when(slot != 0)
                def _():
                    pltpu.make_async_remote_copy(
                        src_ref=away.at[slot],
                        dst_ref=home.at[mine],
                        send_sem=away_sem.at[slot],
                        recv_sem=home_sem.at[mine],
                        device_id=(target, expert),
                        device_id_type=MESH_ID,
                    ).start()

                @pl.when(slot == 0)
                def _():
                    pltpu.make_async_copy(away.at[0], home.at[mine], home_sem.at[mine]).start()

                return c

            lax.fori_loop(0, group, return_one, 0)
            return c

        lax.fori_loop(0, n_dp // group, finish_group, 0)

    def take_home(i, c):
        m = matrix_at(i)
        pltpu.make_async_copy(home.at[m], home.at[m], home_sem.at[m]).wait()
        block = home[m].astype(jnp.float32)
        tiles = [block[:, LANES * tile : LANES * (tile + 1)] for tile in range(MAIN // LANES)]
        for tile, rows in enumerate(unpack_rows(tiles)):
            rows_of(rows32, tile, m, mats)[...] = rows
        return c

    lax.fori_loop(0, mats, take_home, 0)

    def update_row(i, c):
        write(i).wait()
        here = pl.ds(pl.multiple_of(i * mats, 8), mats)
        for tile in range(D // LANES):
            columns = slice(LANES * tile, LANES * (tile + 1))
            out_ref[i, :, columns] = rows32[tile, here, :].astype(jnp.bfloat16)
        return c

    lax.fori_loop(0, ROWS, update_row, 0)

    def sent_done(m, c):
        @pl.when(owner_of(m) != dp)
        def _():
            pltpu.make_async_copy(sent.at[m], sent.at[m], sent_sem.at[m]).wait()

        return c

    lax.fori_loop(0, mats, sent_done, 0)

    @pl.when(owns)
    def _():
        def away_done(slot, c):
            pltpu.make_async_copy(away.at[slot], away.at[slot], away_sem.at[slot]).wait()
            return c

        lax.fori_loop(1, n_dp, away_done, 0)


def orthogonalized(grads, momentum, n_dp):
    mats, height = n_dp // 2, ROWS * n_dp
    group = min(16, n_dp)
    packed = lambda count: pltpu.VMEM((count, TALL, MAIN), jnp.bfloat16)
    flat = lambda *shape: pltpu.VMEM(shape, jnp.bfloat16)
    return pl.pallas_call(
        partial(kernel, n_dp),
        out_shape=[
            jax.ShapeDtypeStruct(grads.shape, jnp.bfloat16),
            jax.ShapeDtypeStruct(grads.shape, jnp.float32),
        ],
        in_specs=[pl.BlockSpec(memory_space=pltpu.HBM)] * 2,
        out_specs=[
            pl.BlockSpec(memory_space=pltpu.VMEM),
            pl.BlockSpec(memory_space=pltpu.HBM),
        ],
        scratch_shapes=[
            pltpu.VMEM(grads.shape, jnp.bfloat16),
            pltpu.VMEM(grads.shape, jnp.float32),
            pltpu.VMEM((D // LANES, ROWS * mats, LANES), jnp.float32),
            packed(mats),
            packed(n_dp),
            flat(height, D),
            flat(height, D),
            flat(height, height),
            flat(height, height),
            packed(n_dp),
            packed(mats),
            flat(SPLITS + 1, ROWS * group, TALL * group),
            flat(SPLITS + 1, TALL * group, ROWS * group),
            pltpu.SemaphoreType.DMA((mats,)),
            pltpu.SemaphoreType.DMA((n_dp,)),
            pltpu.SemaphoreType.DMA((n_dp,)),
            pltpu.SemaphoreType.DMA((mats,)),
            pltpu.SemaphoreType.DMA((2, ROWS)),
            pltpu.SemaphoreType.DMA((ROWS,)),
        ],
        compiler_params=pltpu.CompilerParams(
            collective_id=0, has_side_effects=True, vmem_limit_bytes=VMEM_MIB * 1024 * 1024
        ),
        cost_estimate=pl.CostEstimate(
            flops=8 * height * height * D, bytes_accessed=8 * grads.size, transcendentals=0
        ),
    )(grads, momentum)


def local(grads, momentum):
    n_dp = lax.axis_size("dp")
    swap = lambda array: jnp.transpose(array, (1, 0, 2))
    update, new_momentum = orthogonalized(swap(grads), swap(momentum), n_dp)
    return (swap(update), swap(new_momentum))


def solution(mesh):
    in_specs = (P("expert", "dp", None), P("expert", "dp", None))
    out_specs = (P("expert", "dp", None), P("expert", "dp", None))
    return jax.shard_map(local, mesh=mesh, in_specs=in_specs, out_specs=out_specs, check_vma=False)
```

```python
from functools import partial
import math

import jax
import jax.numpy as jnp
from jax import lax
from jax.experimental import pallas as pl
from jax.experimental.pallas import tpu as pltpu
from jax.sharding import PartitionSpec as P

H = 768
D = 1024
ITERS = 2

A_COEF = 3.4445
B_COEF = -4.775
C_COEF = 2.0315
MOMENT = 0.95
EPS = 1e-07

ROWS = 12
TALL = 16
MAIN = D * ROWS // TALL
EXTRA = D - MAIN
LANES = 128
REST = TALL - ROWS
SPLITS = ROWS // REST
SIDES_Y = 4
BATCHES = 2
MESH_ID = pl.DeviceIdType.MESH


def rows_of(ref, tile, matrix, mats):
    return ref.at[tile, pl.ds(matrix, ROWS, stride=mats), :]


def pack_rows(tiles):
    for tile in range(MAIN // LANES):
        part, side = tile // 2, tile % 2
        below = tiles[MAIN // LANES + side][REST * part : REST * (part + 1)]
        yield jnp.concatenate([tiles[tile], below], axis=0)


def unpack_rows(tiles):
    for tile in range(MAIN // LANES):
        yield tiles[tile][:ROWS]
    for side in range(EXTRA // LANES):
        yield jnp.concatenate([tiles[2 * part + side][ROWS:] for part in range(SPLITS)], axis=0)


def middle_out(i, count):
    sign = 1 - 2 * (i % 2)
    return (count // 2 + sign * ((i + 1) // 2) + count) % count


def selector(plain_dim, packed_dim, shape, part):
    plain = lax.broadcasted_iota(jnp.int32, shape, plain_dim)
    packed = lax.broadcasted_iota(jnp.int32, shape, packed_dim)
    slot = (plain * 43691) >> 19
    row = plain - ROWS * slot
    if part is None:
        hit = packed == TALL * slot + row
    else:
        within = row - REST * part
        hit = (packed == TALL * slot + ROWS + within) & (within >= 0) & (within < REST)
    return jnp.where(hit, 1.0, 0.0).astype(jnp.bfloat16)


def dot(a, b):
    return jnp.dot(a, b, preferred_element_type=jnp.float32)


def dot_t(a, b):
    return lax.dot_general(a, b, (((1,), (1,)), ((), ())), preferred_element_type=jnp.float32)


def kernel(
    n_dp,
    grads_ref,
    mom_ref,
    out_ref,
    new_mom_ref,
    rows32,
    sent,
    landed,
    x0,
    x1,
    gram,
    mixer,
    away,
    home,
    sel,
    sel_t,
    sent_sem,
    landed_sem,
    away_sem,
    home_sem,
):
    n_z = n_dp // SIDES_Y
    mats = n_dp // 2
    height = ROWS * n_dp
    group = min(16, n_dp)
    plain_rows, packed_rows = ROWS * group, TALL * group
    block = 256 if height % 256 == 0 else 128

    def send_to(target, src, dst, send_sem, recv_sem):
        copy = pltpu.make_async_remote_copy(
            src_ref=src,
            dst_ref=dst,
            send_sem=send_sem,
            recv_sem=recv_sem,
            device_id=(target, expert),
            device_id_type=MESH_ID,
        )

        @pl.when(target != dp)
        def _():
            copy.start()

    dp = lax.axis_index("dp")
    expert = lax.axis_index("expert")
    core = expert % 2
    y, z = dp // n_z, dp % n_z
    owns = y % 2 == core
    mine = (y // 2) * n_z + z

    def owner_of(matrix):
        return (core + 2 * (matrix // n_z)) * n_z + matrix % n_z

    barrier = pltpu.get_barrier_semaphore()

    def greet_owner(i, c):
        other = owner_of(i)

        @pl.when(other != dp)
        def _():
            pl.semaphore_signal(barrier, inc=1, device_id=(other, expert), device_id_type=MESH_ID)

        return c

    lax.fori_loop(0, mats, greet_owner, 0)

    @pl.when(owns)
    def _():
        def greet_rest(i, c):
            other = (1 - core + 2 * (i // n_z)) * n_z + i % n_z
            pl.semaphore_signal(barrier, inc=1, device_id=(other, expert), device_id_type=MESH_ID)
            return c

        lax.fori_loop(0, mats, greet_rest, 0)

    def momentum_row(i, c):
        gradient = grads_ref[i].astype(jnp.float32)
        momentum = MOMENT * mom_ref[i] + gradient
        new_mom_ref[i] = momentum
        nesterov = gradient + MOMENT * momentum
        here = pl.ds(pl.multiple_of(i * mats, 8), mats)
        for tile in range(D // LANES):
            rows32[tile, here, :] = nesterov[:, LANES * tile : LANES * (tile + 1)]
        return c

    lax.fori_loop(0, ROWS, momentum_row, 0)

    @pl.when(owns)
    def _():
        pl.semaphore_wait(barrier, n_dp - 1)

    @pl.when(jnp.logical_not(owns))
    def _():
        pl.semaphore_wait(barrier, mats)

    def matrix_at(i):
        batch, turn = i // (mats // BATCHES), i % (mats // BATCHES)
        side = turn % 2
        first_z = z - z % BATCHES + (batch + core) % BATCHES
        return side * n_z + (first_z + BATCHES * middle_out(turn // 2, n_z // BATCHES)) % n_z

    def send_one(i, c):
        m = matrix_at(i)
        owner = owner_of(m)
        slot = (dp - owner + n_dp) % n_dp
        tiles = [rows_of(rows32, tile, m, mats)[...] for tile in range(D // LANES)]
        for tile, block in enumerate(pack_rows(tiles)):
            sent[m, :, LANES * tile : LANES * (tile + 1)] = block.astype(jnp.bfloat16)

        send_to(owner, sent.at[m], landed.at[slot], sent_sem.at[m], landed_sem.at[slot])

        @pl.when(owner == dp)
        def _():
            pltpu.make_async_copy(sent.at[m], landed.at[0], landed_sem.at[0]).start()

        return c

    lax.fori_loop(0, mats, send_one, 0)

    @pl.when(owns)
    def _():
        for part in range(SPLITS + 1):
            which = None if part == 0 else part - 1
            sel[part] = selector(0, 1, (plain_rows, packed_rows), which)
            sel_t[part] = selector(1, 0, (packed_rows, plain_rows), which)

        def unpack_group(g, total):
            def squares(t, total):
                slot = g * group + t
                block = landed.at[slot]
                pltpu.make_async_copy(block, block, landed_sem.at[slot]).wait()
                values = block[...].astype(jnp.float32)
                return total + values * values

            total = lax.fori_loop(0, group, squares, total)
            block = landed[pl.ds(pl.multiple_of(g * group, group), group)]
            block = block.reshape(packed_rows, MAIN)
            rows = pl.ds(pl.multiple_of(g * plain_rows, 16), plain_rows)
            x0[rows, :MAIN] = dot(sel[0], block).astype(jnp.bfloat16)
            tail = dot(sel[1], block[:, :EXTRA])
            for part in range(1, SPLITS):
                tail = tail + dot(sel[part + 1], block[:, EXTRA * part : EXTRA * (part + 1)])
            x0[rows, MAIN:] = tail.astype(jnp.bfloat16)
            return total

        total = jnp.zeros((TALL, MAIN), jnp.float32)
        total = lax.fori_loop(0, n_dp // group, unpack_group, total)
        norm = jnp.sqrt(jnp.sum(total, axis=(0, 1), keepdims=True)) + EPS
        scale_in = 1.0 / norm

        def start_rows(r, c):
            rows = pl.ds(pl.multiple_of(r * plain_rows, 16), plain_rows)
            x0[rows] = (x0[rows].astype(jnp.float32) * scale_in).astype(jnp.bfloat16)
            return c

        lax.fori_loop(0, n_dp // group, start_rows, 0)

        state = x0
        for step in range(ITERS):

            def gram_columns(r, c, state=state):
                part = pl.ds(pl.multiple_of(r * block, 128), block)
                gram[:, part] = dot_t(state[...], state[part]).astype(jnp.bfloat16)
                return c

            def mixer_columns(r, c):
                part = pl.ds(pl.multiple_of(r * block, 128), block)
                some = gram[:, part]
                mixed = B_COEF * some.astype(jnp.float32) + C_COEF * dot(gram[...], some)
                mixer[:, part] = mixed.astype(jnp.bfloat16)
                return c

            lax.fori_loop(0, height // block, gram_columns, 0)
            lax.fori_loop(0, height // block, mixer_columns, 0)

            if step < ITERS - 1:

                def next_columns(r, c, state=state):
                    part = pl.ds(pl.multiple_of(r * block, 128), block)
                    some = state[:, part]
                    moved = dot(mixer[...], some)
                    x1[:, part] = (A_COEF * some.astype(jnp.float32) + moved).astype(jnp.bfloat16)
                    return c

                lax.fori_loop(0, D // block, next_columns, 0)
                state = x1

        scale = 0.2 * math.sqrt(max(H, D))

        def finish_group(g, c):
            rows = pl.ds(pl.multiple_of(g * plain_rows, 16), plain_rows)
            moved = dot(mixer[rows], state[...])
            ortho = (A_COEF * state[rows].astype(jnp.float32) + moved).astype(jnp.bfloat16)
            update = (scale * ortho.astype(jnp.float32)).astype(jnp.bfloat16)
            slots = pl.ds(pl.multiple_of(g * group, group), group)
            for part in range(SPLITS):
                columns = slice(EXTRA * part, EXTRA * (part + 1))
                block = dot(sel_t[0], update[:, columns]) + dot(sel_t[part + 1], update[:, MAIN:])
                away[slots, :, columns] = block.astype(jnp.bfloat16).reshape(group, TALL, EXTRA)

            def return_one(t, c):
                slot = g * group + middle_out(t, group)
                target = (dp + slot) % n_dp

                send_to(
                    target, away.at[slot], home.at[mine], away_sem.at[slot], home_sem.at[mine]
                )

                @pl.when(slot == 0)
                def _():
                    pltpu.make_async_copy(away.at[0], home.at[mine], home_sem.at[mine]).start()

                return c

            lax.fori_loop(0, group, return_one, 0)
            return c

        lax.fori_loop(0, n_dp // group, finish_group, 0)

    def take_home(i, c):
        m = matrix_at(i)
        pltpu.make_async_copy(home.at[m], home.at[m], home_sem.at[m]).wait()
        block = home[m].astype(jnp.float32)
        tiles = [block[:, LANES * tile : LANES * (tile + 1)] for tile in range(MAIN // LANES)]
        for tile, rows in enumerate(unpack_rows(tiles)):
            rows_of(rows32, tile, m, mats)[...] = rows
        return c

    lax.fori_loop(0, mats, take_home, 0)

    def update_row(i, c):
        here = pl.ds(pl.multiple_of(i * mats, 8), mats)
        for tile in range(D // LANES):
            columns = slice(LANES * tile, LANES * (tile + 1))
            out_ref[i, :, columns] = rows32[tile, here, :].astype(jnp.bfloat16)
        return c

    lax.fori_loop(0, ROWS, update_row, 0)

    def sent_done(m, c):
        @pl.when(owner_of(m) != dp)
        def _():
            pltpu.make_async_copy(sent.at[m], sent.at[m], sent_sem.at[m]).wait()

        return c

    lax.fori_loop(0, mats, sent_done, 0)

    @pl.when(owns)
    def _():
        def away_done(slot, c):
            pltpu.make_async_copy(away.at[slot], away.at[slot], away_sem.at[slot]).wait()
            return c

        lax.fori_loop(1, n_dp, away_done, 0)


def orthogonalized(grads, momentum, n_dp):
    mats, height = n_dp // 2, ROWS * n_dp
    group = min(16, n_dp)
    packed = lambda count: pltpu.VMEM((count, TALL, MAIN), jnp.bfloat16)
    flat = lambda *shape: pltpu.VMEM(shape, jnp.bfloat16)
    return pl.pallas_call(
        partial(kernel, n_dp),
        out_shape=[
            jax.ShapeDtypeStruct(grads.shape, jnp.bfloat16),
            jax.ShapeDtypeStruct(grads.shape, jnp.float32),
        ],
        in_specs=[pl.BlockSpec(memory_space=pltpu.VMEM)] * 2,
        out_specs=[pl.BlockSpec(memory_space=pltpu.VMEM)] * 2,
        scratch_shapes=[
            pltpu.VMEM((D // LANES, ROWS * mats, LANES), jnp.float32),
            packed(mats),
            packed(n_dp),
            flat(height, D),
            flat(height, D),
            flat(height, height),
            flat(height, height),
            packed(n_dp),
            packed(mats),
            flat(SPLITS + 1, ROWS * group, TALL * group),
            flat(SPLITS + 1, TALL * group, ROWS * group),
            pltpu.SemaphoreType.DMA((mats,)),
            pltpu.SemaphoreType.DMA((n_dp,)),
            pltpu.SemaphoreType.DMA((n_dp,)),
            pltpu.SemaphoreType.DMA((mats,)),
        ],
        compiler_params=pltpu.CompilerParams(
            collective_id=0, has_side_effects=True, vmem_limit_bytes=40 * 1024 * 1024
        ),
        cost_estimate=pl.CostEstimate(
            flops=8 * height * height * D, bytes_accessed=8 * grads.size, transcendentals=0
        ),
    )(grads, momentum)


def local(grads, momentum):
    n_dp = lax.axis_size("dp")
    swap = lambda array: jnp.transpose(array, (1, 0, 2))
    update, new_momentum = orthogonalized(swap(grads), swap(momentum), n_dp)
    return (swap(update), swap(new_momentum))


def solution(mesh):
    in_specs = (P("expert", "dp", None), P("expert", "dp", None))
    out_specs = (P("expert", "dp", None), P("expert", "dp", None))
    return jax.shard_map(local, mesh=mesh, in_specs=in_specs, out_specs=out_specs, check_vma=False)
```

```python
from functools import partial
import math

import jax
import jax.numpy as jnp
from jax import lax
from jax.experimental import pallas as pl
from jax.experimental.pallas import tpu as pltpu
from jax.sharding import PartitionSpec as P

H = 768
D = 1024
ITERS = 2

A_COEF = 3.4445
B_COEF = -4.775
C_COEF = 2.0315
MOMENT = 0.95
EPS = 1e-07

ROWS = 12
TALL = 16
MAIN = D * ROWS // TALL
EXTRA = D - MAIN
LANES = 128
REST = TALL - ROWS
SPLITS = ROWS // REST
SIDES_Y = 4
BATCHES = 4
MESH_ID = pl.DeviceIdType.MESH


def rows_of(ref, tile, matrix, mats):
    return ref.at[tile, pl.ds(matrix, ROWS, stride=mats), :]


def pack_rows(tiles):
    for tile in range(MAIN // LANES):
        part, side = tile // 2, tile % 2
        below = tiles[MAIN // LANES + side][REST * part : REST * (part + 1)]
        yield jnp.concatenate([tiles[tile], below], axis=0)


def unpack_rows(tiles):
    for tile in range(MAIN // LANES):
        yield tiles[tile][:ROWS]
    for side in range(EXTRA // LANES):
        yield jnp.concatenate([tiles[2 * part + side][ROWS:] for part in range(SPLITS)], axis=0)


def middle_out(i, count):
    sign = 1 - 2 * (i % 2)
    return (count // 2 + sign * ((i + 1) // 2) + count) % count


def selector(plain_dim, packed_dim, shape, part):
    plain = lax.broadcasted_iota(jnp.int32, shape, plain_dim)
    packed = lax.broadcasted_iota(jnp.int32, shape, packed_dim)
    slot = (plain * 43691) >> 19
    row = plain - ROWS * slot
    if part is None:
        hit = packed == TALL * slot + row
    else:
        within = row - REST * part
        hit = (packed == TALL * slot + ROWS + within) & (within >= 0) & (within < REST)
    return jnp.where(hit, 1.0, 0.0).astype(jnp.bfloat16)


def dot(a, b):
    return jnp.dot(a, b, preferred_element_type=jnp.float32)


def dot_t(a, b):
    return lax.dot_general(a, b, (((1,), (1,)), ((), ())), preferred_element_type=jnp.float32)


def kernel(
    n_dp,
    grads_ref,
    mom_ref,
    out_ref,
    new_mom_ref,
    rows32,
    sent,
    landed,
    x0,
    x1,
    gram,
    mixer,
    away,
    home,
    sel,
    sel_t,
    sent_sem,
    landed_sem,
    away_sem,
    home_sem,
):
    n_z = n_dp // SIDES_Y
    mats = n_dp // 2
    height = ROWS * n_dp
    group = min(16, n_dp)
    plain_rows, packed_rows = ROWS * group, TALL * group
    block = 256 if height % 256 == 0 else 128

    def send_to(target, src, dst, send_sem, recv_sem):
        copy = pltpu.make_async_remote_copy(
            src_ref=src,
            dst_ref=dst,
            send_sem=send_sem,
            recv_sem=recv_sem,
            device_id=(target, expert),
            device_id_type=MESH_ID,
        )

        @pl.when(target != dp)
        def _():
            copy.start()

    dp = lax.axis_index("dp")
    expert = lax.axis_index("expert")
    core = expert % 2
    y, z = dp // n_z, dp % n_z
    owns = y % 2 == core
    mine = (y // 2) * n_z + z

    def owner_of(matrix):
        return (core + 2 * (matrix // n_z)) * n_z + matrix % n_z

    barrier = pltpu.get_barrier_semaphore()

    def greet_owner(i, c):
        other = owner_of(i)

        @pl.when(other != dp)
        def _():
            pl.semaphore_signal(barrier, inc=1, device_id=(other, expert), device_id_type=MESH_ID)

        return c

    lax.fori_loop(0, mats, greet_owner, 0)

    @pl.when(owns)
    def _():
        def greet_rest(i, c):
            other = (1 - core + 2 * (i // n_z)) * n_z + i % n_z
            pl.semaphore_signal(barrier, inc=1, device_id=(other, expert), device_id_type=MESH_ID)
            return c

        lax.fori_loop(0, mats, greet_rest, 0)

    def momentum_row(i, c):
        gradient = grads_ref[i].astype(jnp.float32)
        momentum = MOMENT * mom_ref[i] + gradient
        new_mom_ref[i] = momentum
        nesterov = gradient + MOMENT * momentum
        here = pl.ds(pl.multiple_of(i * mats, 8), mats)
        for tile in range(D // LANES):
            rows32[tile, here, :] = nesterov[:, LANES * tile : LANES * (tile + 1)]
        return c

    lax.fori_loop(0, ROWS, momentum_row, 0)

    @pl.when(owns)
    def _():
        pl.semaphore_wait(barrier, n_dp - 1)

    @pl.when(jnp.logical_not(owns))
    def _():
        pl.semaphore_wait(barrier, mats)

    def matrix_at(i):
        batch, turn = i // (mats // BATCHES), i % (mats // BATCHES)
        side = turn % 2
        first_z = z - z % BATCHES + (batch + core + 2 * side) % BATCHES
        return side * n_z + (first_z + BATCHES * middle_out(turn // 2, n_z // BATCHES)) % n_z

    def send_one(i, c):
        m = matrix_at(i)
        owner = owner_of(m)
        slot = (dp - owner + n_dp) % n_dp
        tiles = [rows_of(rows32, tile, m, mats)[...] for tile in range(D // LANES)]
        for tile, block in enumerate(pack_rows(tiles)):
            sent[m, :, LANES * tile : LANES * (tile + 1)] = block.astype(jnp.bfloat16)

        send_to(owner, sent.at[m], landed.at[slot], sent_sem.at[m], landed_sem.at[slot])

        @pl.when(owner == dp)
        def _():
            pltpu.make_async_copy(sent.at[m], landed.at[0], landed_sem.at[0]).start()

        return c

    lax.fori_loop(0, mats, send_one, 0)

    @pl.when(owns)
    def _():
        for part in range(SPLITS + 1):
            which = None if part == 0 else part - 1
            sel[part] = selector(0, 1, (plain_rows, packed_rows), which)
            sel_t[part] = selector(1, 0, (packed_rows, plain_rows), which)

        def unpack_group(g, total):
            def squares(t, total):
                slot = g * group + t
                block = landed.at[slot]
                pltpu.make_async_copy(block, block, landed_sem.at[slot]).wait()
                values = block[...].astype(jnp.float32)
                return total + values * values

            total = lax.fori_loop(0, group, squares, total)
            block = landed[pl.ds(pl.multiple_of(g * group, group), group)]
            block = block.reshape(packed_rows, MAIN)
            rows = pl.ds(pl.multiple_of(g * plain_rows, 16), plain_rows)
            x0[rows, :MAIN] = dot(sel[0], block).astype(jnp.bfloat16)
            tail = dot(sel[1], block[:, :EXTRA])
            for part in range(1, SPLITS):
                tail = tail + dot(sel[part + 1], block[:, EXTRA * part : EXTRA * (part + 1)])
            x0[rows, MAIN:] = tail.astype(jnp.bfloat16)
            return total

        total = jnp.zeros((TALL, MAIN), jnp.float32)
        total = lax.fori_loop(0, n_dp // group, unpack_group, total)
        norm = jnp.sqrt(jnp.sum(total, axis=(0, 1), keepdims=True)) + EPS
        scale_in = 1.0 / norm

        def start_rows(r, c):
            rows = pl.ds(pl.multiple_of(r * plain_rows, 16), plain_rows)
            x0[rows] = (x0[rows].astype(jnp.float32) * scale_in).astype(jnp.bfloat16)
            return c

        lax.fori_loop(0, n_dp // group, start_rows, 0)

        state = x0
        for step in range(ITERS):

            def gram_columns(r, c, state=state):
                part = pl.ds(pl.multiple_of(r * block, 128), block)
                gram[:, part] = dot_t(state[...], state[part]).astype(jnp.bfloat16)
                return c

            def mixer_columns(r, c):
                part = pl.ds(pl.multiple_of(r * block, 128), block)
                some = gram[:, part]
                mixed = B_COEF * some.astype(jnp.float32) + C_COEF * dot(gram[...], some)
                mixer[:, part] = mixed.astype(jnp.bfloat16)
                return c

            lax.fori_loop(0, height // block, gram_columns, 0)
            lax.fori_loop(0, height // block, mixer_columns, 0)

            if step < ITERS - 1:

                def next_columns(r, c, state=state):
                    part = pl.ds(pl.multiple_of(r * block, 128), block)
                    some = state[:, part]
                    moved = dot(mixer[...], some)
                    x1[:, part] = (A_COEF * some.astype(jnp.float32) + moved).astype(jnp.bfloat16)
                    return c

                lax.fori_loop(0, D // block, next_columns, 0)
                state = x1

        scale = 0.2 * math.sqrt(max(H, D))

        def finish_group(g, c):
            rows = pl.ds(pl.multiple_of(g * plain_rows, 16), plain_rows)
            moved = dot(mixer[rows], state[...])
            ortho = (A_COEF * state[rows].astype(jnp.float32) + moved).astype(jnp.bfloat16)
            update = (scale * ortho.astype(jnp.float32)).astype(jnp.bfloat16)
            slots = pl.ds(pl.multiple_of(g * group, group), group)
            for part in range(SPLITS):
                columns = slice(EXTRA * part, EXTRA * (part + 1))
                block = dot(sel_t[0], update[:, columns]) + dot(sel_t[part + 1], update[:, MAIN:])
                away[slots, :, columns] = block.astype(jnp.bfloat16).reshape(group, TALL, EXTRA)

            def return_one(t, c):
                slot = g * group + middle_out(t, group)
                target = (dp + slot) % n_dp

                send_to(
                    target, away.at[slot], home.at[mine], away_sem.at[slot], home_sem.at[mine]
                )

                @pl.when(slot == 0)
                def _():
                    pltpu.make_async_copy(away.at[0], home.at[mine], home_sem.at[mine]).start()

                return c

            lax.fori_loop(0, group, return_one, 0)
            return c

        lax.fori_loop(0, n_dp // group, finish_group, 0)

    def take_home(i, c):
        m = matrix_at(i)
        pltpu.make_async_copy(home.at[m], home.at[m], home_sem.at[m]).wait()
        block = home[m].astype(jnp.float32)
        tiles = [block[:, LANES * tile : LANES * (tile + 1)] for tile in range(MAIN // LANES)]
        for tile, rows in enumerate(unpack_rows(tiles)):
            rows_of(rows32, tile, m, mats)[...] = rows
        return c

    lax.fori_loop(0, mats, take_home, 0)

    def update_row(i, c):
        here = pl.ds(pl.multiple_of(i * mats, 8), mats)
        for tile in range(D // LANES):
            columns = slice(LANES * tile, LANES * (tile + 1))
            out_ref[i, :, columns] = rows32[tile, here, :].astype(jnp.bfloat16)
        return c

    lax.fori_loop(0, ROWS, update_row, 0)

    def sent_done(m, c):
        @pl.when(owner_of(m) != dp)
        def _():
            pltpu.make_async_copy(sent.at[m], sent.at[m], sent_sem.at[m]).wait()

        return c

    lax.fori_loop(0, mats, sent_done, 0)

    @pl.when(owns)
    def _():
        def away_done(slot, c):
            pltpu.make_async_copy(away.at[slot], away.at[slot], away_sem.at[slot]).wait()
            return c

        lax.fori_loop(1, n_dp, away_done, 0)


def orthogonalized(grads, momentum, n_dp):
    mats, height = n_dp // 2, ROWS * n_dp
    group = min(16, n_dp)
    packed = lambda count: pltpu.VMEM((count, TALL, MAIN), jnp.bfloat16)
    flat = lambda *shape: pltpu.VMEM(shape, jnp.bfloat16)
    return pl.pallas_call(
        partial(kernel, n_dp),
        out_shape=[
            jax.ShapeDtypeStruct(grads.shape, jnp.bfloat16),
            jax.ShapeDtypeStruct(grads.shape, jnp.float32),
        ],
        in_specs=[pl.BlockSpec(memory_space=pltpu.VMEM)] * 2,
        out_specs=[pl.BlockSpec(memory_space=pltpu.VMEM)] * 2,
        scratch_shapes=[
            pltpu.VMEM((D // LANES, ROWS * mats, LANES), jnp.float32),
            packed(mats),
            packed(n_dp),
            flat(height, D),
            flat(height, D),
            flat(height, height),
            flat(height, height),
            packed(n_dp),
            packed(mats),
            flat(SPLITS + 1, ROWS * group, TALL * group),
            flat(SPLITS + 1, TALL * group, ROWS * group),
            pltpu.SemaphoreType.DMA((mats,)),
            pltpu.SemaphoreType.DMA((n_dp,)),
            pltpu.SemaphoreType.DMA((n_dp,)),
            pltpu.SemaphoreType.DMA((mats,)),
        ],
        compiler_params=pltpu.CompilerParams(
            collective_id=0, has_side_effects=True, vmem_limit_bytes=40 * 1024 * 1024
        ),
        cost_estimate=pl.CostEstimate(
            flops=8 * height * height * D, bytes_accessed=8 * grads.size, transcendentals=0
        ),
    )(grads, momentum)


def local(grads, momentum):
    n_dp = lax.axis_size("dp")
    swap = lambda array: jnp.transpose(array, (1, 0, 2))
    update, new_momentum = orthogonalized(swap(grads), swap(momentum), n_dp)
    return (swap(update), swap(new_momentum))


def solution(mesh):
    in_specs = (P("expert", "dp", None), P("expert", "dp", None))
    out_specs = (P("expert", "dp", None), P("expert", "dp", None))
    return jax.shard_map(local, mesh=mesh, in_specs=in_specs, out_specs=out_specs, check_vma=False)
```

```python
from functools import partial
import math

import jax
import jax.numpy as jnp
from jax import lax
from jax.experimental import pallas as pl
from jax.experimental.pallas import tpu as pltpu
from jax.sharding import PartitionSpec as P

H = 768
D = 1024
ITERS = 2

A_COEF = 3.4445
B_COEF = -4.775
C_COEF = 2.0315
MOMENT = 0.95
EPS = 1e-07

ROWS = 12
TALL = 16
MAIN = D * ROWS // TALL
EXTRA = D - MAIN
LANES = 128
REST = TALL - ROWS
SPLITS = ROWS // REST
SIDES_Y = 4
BATCHES = 4
VMEM_MIB = 53
MESH_ID = pl.DeviceIdType.MESH


def rows_of(ref, tile, matrix, mats):
    return ref.at[tile, pl.ds(matrix, ROWS, stride=mats), :]


def pack_rows(tiles):
    for tile in range(MAIN // LANES):
        part, side = tile // 2, tile % 2
        below = tiles[MAIN // LANES + side][REST * part : REST * (part + 1)]
        yield jnp.concatenate([tiles[tile], below], axis=0)


def unpack_rows(tiles):
    for tile in range(MAIN // LANES):
        yield tiles[tile][:ROWS]
    for side in range(EXTRA // LANES):
        yield jnp.concatenate([tiles[2 * part + side][ROWS:] for part in range(SPLITS)], axis=0)


def middle_out(i, count):
    sign = 1 - 2 * (i % 2)
    return (count // 2 + sign * ((i + 1) // 2) + count) % count


def selector(plain_dim, packed_dim, shape, part):
    plain = lax.broadcasted_iota(jnp.int32, shape, plain_dim)
    packed = lax.broadcasted_iota(jnp.int32, shape, packed_dim)
    slot = (plain * 43691) >> 19
    row = plain - ROWS * slot
    if part is None:
        hit = packed == TALL * slot + row
    else:
        within = row - REST * part
        hit = (packed == TALL * slot + ROWS + within) & (within >= 0) & (within < REST)
    return jnp.where(hit, 1.0, 0.0).astype(jnp.bfloat16)


def dot(a, b):
    return jnp.dot(a, b, preferred_element_type=jnp.float32)


def dot_t(a, b):
    return lax.dot_general(a, b, (((1,), (1,)), ((), ())), preferred_element_type=jnp.float32)


def kernel(
    n_dp,
    grads_hbm,
    mom_hbm,
    out_ref,
    new_mom_hbm,
    grads_ref,
    mom_ref,
    rows32,
    sent,
    landed,
    x0,
    x1,
    gram,
    mixer,
    away,
    home,
    sel,
    sel_t,
    sent_sem,
    landed_sem,
    away_sem,
    home_sem,
    read_sem,
    write_sem,
):
    n_z = n_dp // SIDES_Y
    mats = n_dp // 2
    height = ROWS * n_dp
    group = min(16, n_dp)
    plain_rows, packed_rows = ROWS * group, TALL * group
    block = 256 if height % 256 == 0 else 128

    def send_to(target, src, dst, send_sem, recv_sem):
        copy = pltpu.make_async_remote_copy(
            src_ref=src,
            dst_ref=dst,
            send_sem=send_sem,
            recv_sem=recv_sem,
            device_id=(target, expert),
            device_id_type=MESH_ID,
        )

        @pl.when(target != dp)
        def _():
            copy.start()

    dp = lax.axis_index("dp")
    expert = lax.axis_index("expert")
    core = expert % 2
    y, z = dp // n_z, dp % n_z
    owns = y % 2 == core
    mine = (y // 2) * n_z + z

    def owner_of(matrix):
        return (core + 2 * (matrix // n_z)) * n_z + matrix % n_z

    def read(i):
        yield pltpu.make_async_copy(mom_hbm.at[i], mom_ref.at[i], read_sem.at[0, i])
        yield pltpu.make_async_copy(grads_hbm.at[i], grads_ref.at[i], read_sem.at[1, i])

    def write(i):
        return pltpu.make_async_copy(mom_ref.at[i], new_mom_hbm.at[i], write_sem.at[i])

    def start_read(i, c):
        for copy in read(i):
            copy.start()
        return c

    lax.fori_loop(0, ROWS, start_read, 0)

    barrier = pltpu.get_barrier_semaphore()

    def greet_owner(i, c):
        other = owner_of(i)

        @pl.when(other != dp)
        def _():
            pl.semaphore_signal(barrier, inc=1, device_id=(other, expert), device_id_type=MESH_ID)

        return c

    lax.fori_loop(0, mats, greet_owner, 0)

    @pl.when(owns)
    def _():
        def greet_rest(i, c):
            other = (1 - core + 2 * (i // n_z)) * n_z + i % n_z
            pl.semaphore_signal(barrier, inc=1, device_id=(other, expert), device_id_type=MESH_ID)
            return c

        lax.fori_loop(0, mats, greet_rest, 0)

    def momentum_row(i, c):
        for copy in read(i):
            copy.wait()
        gradient = grads_ref[i].astype(jnp.float32)
        momentum = MOMENT * mom_ref[i] + gradient
        mom_ref[i] = momentum
        write(i).start()
        nesterov = gradient + MOMENT * momentum
        here = pl.ds(pl.multiple_of(i * mats, 8), mats)
        for tile in range(D // LANES):
            rows32[tile, here, :] = nesterov[:, LANES * tile : LANES * (tile + 1)]
        return c

    lax.fori_loop(0, ROWS, momentum_row, 0)

    @pl.when(owns)
    def _():
        pl.semaphore_wait(barrier, n_dp - 1)

    @pl.when(jnp.logical_not(owns))
    def _():
        pl.semaphore_wait(barrier, mats)

    def matrix_at(i):
        batch, turn = i // (mats // BATCHES), i % (mats // BATCHES)
        side = turn % 2
        first_z = z - z % BATCHES + (batch + core + 2 * side) % BATCHES
        return side * n_z + (first_z + BATCHES * middle_out(turn // 2, n_z // BATCHES)) % n_z

    def send_one(i, c):
        m = matrix_at(i)
        owner = owner_of(m)
        slot = (dp - owner + n_dp) % n_dp
        tiles = [rows_of(rows32, tile, m, mats)[...] for tile in range(D // LANES)]
        for tile, block in enumerate(pack_rows(tiles)):
            sent[m, :, LANES * tile : LANES * (tile + 1)] = block.astype(jnp.bfloat16)

        send_to(owner, sent.at[m], landed.at[slot], sent_sem.at[m], landed_sem.at[slot])

        @pl.when(owner == dp)
        def _():
            pltpu.make_async_copy(sent.at[m], landed.at[0], landed_sem.at[0]).start()

        return c

    lax.fori_loop(0, mats, send_one, 0)

    @pl.when(owns)
    def _():
        for part in range(SPLITS + 1):
            which = None if part == 0 else part - 1
            sel[part] = selector(0, 1, (plain_rows, packed_rows), which)
            sel_t[part] = selector(1, 0, (packed_rows, plain_rows), which)

        def unpack_group(g, total):
            def squares(t, total):
                slot = g * group + t
                block = landed.at[slot]
                pltpu.make_async_copy(block, block, landed_sem.at[slot]).wait()
                values = block[...].astype(jnp.float32)
                return total + values * values

            total = lax.fori_loop(0, group, squares, total)
            block = landed[pl.ds(pl.multiple_of(g * group, group), group)]
            block = block.reshape(packed_rows, MAIN)
            rows = pl.ds(pl.multiple_of(g * plain_rows, 16), plain_rows)
            x0[rows, :MAIN] = dot(sel[0], block).astype(jnp.bfloat16)
            tail = dot(sel[1], block[:, :EXTRA])
            for part in range(1, SPLITS):
                tail = tail + dot(sel[part + 1], block[:, EXTRA * part : EXTRA * (part + 1)])
            x0[rows, MAIN:] = tail.astype(jnp.bfloat16)
            return total

        total = jnp.zeros((TALL, MAIN), jnp.float32)
        total = lax.fori_loop(0, n_dp // group, unpack_group, total)
        norm = jnp.sqrt(jnp.sum(total, axis=(0, 1), keepdims=True)) + EPS
        scale_in = 1.0 / norm

        def start_rows(r, c):
            rows = pl.ds(pl.multiple_of(r * plain_rows, 16), plain_rows)
            x0[rows] = (x0[rows].astype(jnp.float32) * scale_in).astype(jnp.bfloat16)
            return c

        lax.fori_loop(0, n_dp // group, start_rows, 0)

        state = x0
        for step in range(ITERS):

            def gram_columns(r, c, state=state):
                part = pl.ds(pl.multiple_of(r * block, 128), block)
                gram[:, part] = dot_t(state[...], state[part]).astype(jnp.bfloat16)
                return c

            def mixer_columns(r, c):
                part = pl.ds(pl.multiple_of(r * block, 128), block)
                some = gram[:, part]
                mixed = B_COEF * some.astype(jnp.float32) + C_COEF * dot(gram[...], some)
                mixer[:, part] = mixed.astype(jnp.bfloat16)
                return c

            lax.fori_loop(0, height // block, gram_columns, 0)
            lax.fori_loop(0, height // block, mixer_columns, 0)

            if step < ITERS - 1:

                def next_columns(r, c, state=state):
                    part = pl.ds(pl.multiple_of(r * block, 128), block)
                    some = state[:, part]
                    moved = dot(mixer[...], some)
                    x1[:, part] = (A_COEF * some.astype(jnp.float32) + moved).astype(jnp.bfloat16)
                    return c

                lax.fori_loop(0, D // block, next_columns, 0)
                state = x1

        scale = 0.2 * math.sqrt(max(H, D))

        def finish_group(g, c):
            rows = pl.ds(pl.multiple_of(g * plain_rows, 16), plain_rows)
            moved = dot(mixer[rows], state[...])
            ortho = (A_COEF * state[rows].astype(jnp.float32) + moved).astype(jnp.bfloat16)
            update = (scale * ortho.astype(jnp.float32)).astype(jnp.bfloat16)
            slots = pl.ds(pl.multiple_of(g * group, group), group)
            for part in range(SPLITS):
                columns = slice(EXTRA * part, EXTRA * (part + 1))
                block = dot(sel_t[0], update[:, columns]) + dot(sel_t[part + 1], update[:, MAIN:])
                away[slots, :, columns] = block.astype(jnp.bfloat16).reshape(group, TALL, EXTRA)

            def return_one(t, c):
                slot = g * group + middle_out(t, group)
                target = (dp + slot) % n_dp

                send_to(
                    target, away.at[slot], home.at[mine], away_sem.at[slot], home_sem.at[mine]
                )

                @pl.when(slot == 0)
                def _():
                    pltpu.make_async_copy(away.at[0], home.at[mine], home_sem.at[mine]).start()

                return c

            lax.fori_loop(0, group, return_one, 0)
            return c

        lax.fori_loop(0, n_dp // group, finish_group, 0)

    def take_home(i, c):
        m = matrix_at(i)
        pltpu.make_async_copy(home.at[m], home.at[m], home_sem.at[m]).wait()
        block = home[m].astype(jnp.float32)
        tiles = [block[:, LANES * tile : LANES * (tile + 1)] for tile in range(MAIN // LANES)]
        for tile, rows in enumerate(unpack_rows(tiles)):
            rows_of(rows32, tile, m, mats)[...] = rows
        return c

    lax.fori_loop(0, mats, take_home, 0)

    def update_row(i, c):
        write(i).wait()
        here = pl.ds(pl.multiple_of(i * mats, 8), mats)
        for tile in range(D // LANES):
            columns = slice(LANES * tile, LANES * (tile + 1))
            out_ref[i, :, columns] = rows32[tile, here, :].astype(jnp.bfloat16)
        return c

    lax.fori_loop(0, ROWS, update_row, 0)

    def sent_done(m, c):
        @pl.when(owner_of(m) != dp)
        def _():
            pltpu.make_async_copy(sent.at[m], sent.at[m], sent_sem.at[m]).wait()

        return c

    lax.fori_loop(0, mats, sent_done, 0)

    @pl.when(owns)
    def _():
        def away_done(slot, c):
            pltpu.make_async_copy(away.at[slot], away.at[slot], away_sem.at[slot]).wait()
            return c

        lax.fori_loop(1, n_dp, away_done, 0)


def orthogonalized(grads, momentum, n_dp):
    mats, height = n_dp // 2, ROWS * n_dp
    group = min(16, n_dp)
    packed = lambda count: pltpu.VMEM((count, TALL, MAIN), jnp.bfloat16)
    flat = lambda *shape: pltpu.VMEM(shape, jnp.bfloat16)
    return pl.pallas_call(
        partial(kernel, n_dp),
        out_shape=[
            jax.ShapeDtypeStruct(grads.shape, jnp.bfloat16),
            jax.ShapeDtypeStruct(grads.shape, jnp.float32),
        ],
        in_specs=[pl.BlockSpec(memory_space=pltpu.HBM)] * 2,
        out_specs=[
            pl.BlockSpec(memory_space=pltpu.VMEM),
            pl.BlockSpec(memory_space=pltpu.HBM),
        ],
        scratch_shapes=[
            pltpu.VMEM(grads.shape, jnp.bfloat16),
            pltpu.VMEM(grads.shape, jnp.float32),
            pltpu.VMEM((D // LANES, ROWS * mats, LANES), jnp.float32),
            packed(mats),
            packed(n_dp),
            flat(height, D),
            flat(height, D),
            flat(height, height),
            flat(height, height),
            packed(n_dp),
            packed(mats),
            flat(SPLITS + 1, ROWS * group, TALL * group),
            flat(SPLITS + 1, TALL * group, ROWS * group),
            pltpu.SemaphoreType.DMA((mats,)),
            pltpu.SemaphoreType.DMA((n_dp,)),
            pltpu.SemaphoreType.DMA((n_dp,)),
            pltpu.SemaphoreType.DMA((mats,)),
            pltpu.SemaphoreType.DMA((2, ROWS)),
            pltpu.SemaphoreType.DMA((ROWS,)),
        ],
        compiler_params=pltpu.CompilerParams(
            collective_id=0, has_side_effects=True, vmem_limit_bytes=VMEM_MIB * 1024 * 1024
        ),
        cost_estimate=pl.CostEstimate(
            flops=8 * height * height * D, bytes_accessed=8 * grads.size, transcendentals=0
        ),
    )(grads, momentum)


def local(grads, momentum):
    n_dp = lax.axis_size("dp")
    swap = lambda array: jnp.transpose(array, (1, 0, 2))
    update, new_momentum = orthogonalized(swap(grads), swap(momentum), n_dp)
    return (swap(update), swap(new_momentum))


def solution(mesh):
    in_specs = (P("expert", "dp", None), P("expert", "dp", None))
    out_specs = (P("expert", "dp", None), P("expert", "dp", None))
    return jax.shard_map(local, mesh=mesh, in_specs=in_specs, out_specs=out_specs, check_vma=False)
```
